32 devices in a mesh: energy: 16 (over z, y, x), space: 2 (over core).
Axes of the slice: x: 2, y: 2, z: 4, core: 2. Of those that a mesh axis runs over, the one named last changes fastest.
Arguments:
- green_ret: bfloat16 [16, 16, 128, 128], P('energy', 'space'), may hold values from -0.5 to 0.5
- prior_less: bfloat16 [16, 16, 128, 128], P('energy', 'space'), may hold values from -1.25 to 9.25
- prior_great: bfloat16 [16, 16, 128, 128], P('energy', 'space'), may hold values from -1.25 to 9.25
- coupling: bfloat16 [16, 128, 128], P('space'), may hold values from -0.5 to 0.5
- phonon_coupling: float32 [128, 128], P('energy'), may hold values from 0.1 to 1
- phonon_shift: int32 [2], replicated, may hold values from 1 to 8
- active_blocks: int32 [16], replicated, may hold values from 8 to 16
Outputs:
- sigma_less: bfloat16 [16, 16, 128, 128], P(None, 'space', 'energy')
- sigma_great: bfloat16 [16, 16, 128, 128], P(None, 'space', 'energy')
- current: float32 [16, 16], P('energy', 'space')
- ldos: float32 [16, 16], P('energy', 'space')
The draws below stay inside these ranges and needn't reach their ends.
All inputs are finite; a program needn't handle non-finite values.
Results may differ from the reference program's by a relative error of at most 0.009.
Values may be sent and summed in bfloat16 or wider, within the bound.
No kernel may reach another device: no remote copies, remote signals or barrier semaphores. Data moves between devices by JAX's collectives and lax.ppermute only.
A program may use at most 64 MiB of HBM per device.

```python
import math
import jax
import jax.numpy as jnp
from jax import lax

B = 128
NE = 16
NB = 16


def prior_block(key):
    first, second = jax.random.split(key)
    noise = jnp.clip(0.3 * jax.random.normal(first, (NE, NB, B, B), jnp.float32), -1.2, 1.2)
    diagonal = jnp.exp(jax.random.uniform(second, (NE, NB, B, 1), jnp.float32, math.log(0.5), math.log(4.0)))
    identity = jnp.eye(B, dtype=jnp.float32)
    return noise + identity * diagonal


def draw_prior_less(key, part):
    return prior_block(jax.random.fold_in(key, 11)).astype(jnp.bfloat16)


def draw_prior_great(key, part):
    return prior_block(jax.random.fold_in(key, 23)).astype(jnp.bfloat16)


def plant(drawn, own_key, low, high):
    place = [jax.random.randint(jax.random.fold_in(own_key, axis), (), 0, length) for axis, length in enumerate(drawn.shape)]
    widest = drawn.shape.index(max(drawn.shape))
    beside = place[:widest] + [(place[widest] + 1) % drawn.shape[widest]] + place[widest + 1:]
    return drawn.at[tuple(place)].set(low).at[tuple(beside)].set(high)


def shard_levels(key, extent, cuts, low, high):
    gain, own = 1.0, jax.random.fold_in(key, 6)
    for dim, blocks in cuts:
        draws = jnp.exp(jax.random.uniform(jax.random.fold_in(own, dim), (blocks,), jnp.float32, low / len(cuts), high / len(cuts)))
        gain = gain * jnp.repeat(draws, extent[dim] // blocks).reshape([-1 if axis == dim else 1 for axis in range(len(extent))])
    return gain


def centred(own_key, shape, width, bound, cuts=(), kind=jnp.bfloat16):
    array = width * jax.random.normal(own_key, shape, jnp.float32)
    if cuts:
        array = array * shard_levels(own_key, shape, cuts, -0.22, 0.18)
    return jnp.clip(array, -bound, bound).astype(kind)


def setup_inputs(seed: int = 0) -> dict:
    seeds = jax.random.split(jax.random.key(seed), 8)
    return {
        "green_ret": centred(seeds[0], (NE, NB, B, B), B ** -0.5, 0.5, ((0, 16), (1, 2))),
        "prior_less": draw_prior_less(jax.random.fold_in(seeds[7], 71), 0),
        "prior_great": draw_prior_great(jax.random.fold_in(seeds[7], 71), 0),
        "coupling": centred(seeds[3], (NB, B, B), B ** -0.5, 0.5, ((0, 2),)),
        "phonon_coupling": jnp.clip(jnp.exp(math.log(1.0) - 2.3025851 * jax.random.uniform(seeds[4], (B, B), jnp.float32) ** shard_levels(seeds[4], (B, B), ((0, 16),), -0.2, 0.2)), 0.1, 1.0),
        "phonon_shift": jax.random.randint(seeds[5], (2,), 1, NE // 2 + 1).astype(jnp.int32),
        "active_blocks": plant(jax.random.randint(seeds[6], (NE,), NB // 2, NB + 1), jax.random.fold_in(seeds[6], 1), NB // 2, NB).astype(jnp.int32),
    }


phonon_occupation = 0.5


def widen(values):
    return values.astype(jnp.float32)


def propagate(retarded, prior, coupling, open_mask):
    half_product = jnp.einsum("nij,njl->nil", widen(retarded), widen(prior)).astype(jnp.bfloat16)
    bare = jnp.einsum("nil,nml->nim", widen(half_product), widen(retarded)).astype(jnp.bfloat16)
    raised = jnp.einsum("nji,njl->nil", widen(coupling), widen(bare)).astype(jnp.bfloat16)
    upward = jnp.einsum("nil,nlm->nim", widen(raised), widen(coupling)).astype(jnp.bfloat16)
    following = jnp.concatenate([bare[1:], jnp.zeros_like(bare[:1])], 0)
    lowered = jnp.einsum("nij,njl->nil", widen(coupling), widen(following)).astype(jnp.bfloat16)
    downward = jnp.einsum("nil,nml->nim", widen(lowered), widen(coupling))
    previous = jnp.concatenate([jnp.zeros_like(upward[:1]), upward[:-1]], 0)
    source = (widen(prior) + widen(previous) + downward).astype(jnp.bfloat16)
    second_half = jnp.einsum("nij,njl->nil", widen(retarded), widen(source)).astype(jnp.bfloat16)
    result = jnp.einsum("nil,nml->nim", widen(second_half), widen(retarded))
    return (result * open_mask[:, None, None]).astype(jnp.bfloat16)


def at_energy(blocks_in, target):
    inside_grid = (target >= 0) & (target < NE)
    clipped = jnp.clip(target, 0, NE - 1).astype(jnp.int32)
    piece = lax.dynamic_index_in_dim(blocks_in, clipped, 0, keepdims=False)
    return jnp.where(inside_grid, widen(piece), jnp.float32(0.0))


def reference(green_ret, prior_less, prior_great, coupling, phonon_coupling, phonon_shift, active_blocks):
    positions = jnp.arange(NB, dtype=jnp.int32)

    def per_energy(inputs):
        retarded, less_part, great_part, open_count = inputs
        open_mask = (positions < open_count).astype(jnp.float32)
        return (propagate(retarded, less_part, coupling, open_mask),
                propagate(retarded, great_part, coupling, open_mask))

    lesser, greater = lax.map(per_energy, (green_ret, prior_less, prior_great, active_blocks))
    diag_mask = jnp.eye(B, dtype=jnp.float32)
    occupied = jnp.float32(phonon_occupation)

    def per_energy_out(energy_index):
        less_sum = jnp.zeros((NB, B, B), jnp.float32)
        great_sum = jnp.zeros((NB, B, B), jnp.float32)
        for branch in range(2):
            offset = phonon_shift[branch]
            less_up = at_energy(lesser, energy_index + offset)
            less_down = at_energy(lesser, energy_index - offset)
            great_up = at_energy(greater, energy_index + offset)
            great_down = at_energy(greater, energy_index - offset)
            less_sum = less_sum + (1.0 + occupied) * less_up + occupied * less_down
            great_sum = great_sum + (1.0 + occupied) * great_down + occupied * great_up
        sigma_l = (phonon_coupling * less_sum).astype(jnp.bfloat16)
        sigma_g = (phonon_coupling * great_sum).astype(jnp.bfloat16)
        lesser_here = at_energy(lesser, energy_index)
        greater_here = at_energy(greater, energy_index)
        scattering = jnp.sum(widen(sigma_l) * greater_here - widen(sigma_g) * lesser_here, axis=(1, 2)) / B
        density = jnp.sum((lesser_here + greater_here) * diag_mask, axis=(1, 2)) / B
        return sigma_l, sigma_g, scattering, density

    sigma_less, sigma_great, current, ldos = lax.map(per_energy_out, jnp.arange(NE, dtype=jnp.int32))
    return (sigma_less, sigma_great, current, ldos)
```

```python
import jax
import jax.numpy as jnp
from jax import lax
from jax.sharding import PartitionSpec as P

phonon_occupation = 0.5


def shifted(value, axis, steps):
    count = lax.axis_size(axis)
    initial, last = (max(0, -steps), min(count, count - steps))
    return lax.ppermute(value, axis, [(source, source + steps) for source in range(initial, last)])


def sandwich(retarded, middle_part):
    half_product = jnp.einsum(
        "enij,kenjl->kenil", retarded, middle_part, preferred_element_type=jnp.float32
    ).astype(jnp.bfloat16)
    return jnp.einsum(
        "kenil,enml->kenim", half_product, retarded, preferred_element_type=jnp.float32
    )


def displaced(blocks_in, offset):
    energies = blocks_in.shape[0]
    target = jnp.arange(energies, dtype=jnp.int32) + offset
    inside_grid = (target >= 0) & (target < energies)
    rolled = jnp.roll(blocks_in, -offset, axis=0).astype(jnp.float32)
    return jnp.where(inside_grid[:, None, None, None], rolled, jnp.float32(0.0))


def local(
    green_ret, prior_less, prior_great, coupling, phonon_coupling, phonon_shift, active_blocks
):
    energy_count, block_count, orbitals, _ = green_ret.shape
    energy_start = lax.axis_index("energy") * energy_count
    block_start = lax.axis_index("space") * block_count
    priors = jnp.stack([prior_less, prior_great])
    bare = sandwich(green_ret, priors).astype(jnp.bfloat16)
    next_first = shifted(bare[:, :, 0], "space", -1)
    following = jnp.concatenate([bare[:, :, 1:], next_first[:, :, None]], 2)
    lowered = jnp.einsum(
        "nij,kenjl->kenil", coupling, following, preferred_element_type=jnp.float32
    ).astype(jnp.bfloat16)
    downward = jnp.einsum("kenil,nml->kenim", lowered, coupling, preferred_element_type=jnp.float32)
    raised = jnp.einsum(
        "nji,kenjl->kenil", coupling, bare, preferred_element_type=jnp.float32
    ).astype(jnp.bfloat16)
    upward = jnp.einsum(
        "kenil,nlm->kenim", raised, coupling, preferred_element_type=jnp.float32
    ).astype(jnp.bfloat16)
    prev_upward = shifted(upward[:, :, -1], "space", 1)
    previous = jnp.concatenate([prev_upward[:, :, None], upward[:, :, :-1]], 2)
    source = (priors.astype(jnp.float32) + previous.astype(jnp.float32) + downward).astype(
        jnp.bfloat16
    )
    result = sandwich(green_ret, source)
    open_counts = lax.dynamic_slice_in_dim(active_blocks, energy_start, energy_count)
    block_ids = block_start + jnp.arange(block_count, dtype=jnp.int32)
    open_mask = (block_ids[None, :] < open_counts[:, None]).astype(jnp.float32)
    greens = (result * open_mask[None, :, :, None, None]).astype(jnp.bfloat16)
    devices = lax.axis_size("energy")
    row_count = orbitals // devices
    occupied = jnp.float32(phonon_occupation)
    identity = jnp.eye(orbitals, dtype=jnp.float32)
    density = jnp.sum(greens.astype(jnp.float32) * identity, axis=(0, 3, 4)) / orbitals
    outgoing = greens.reshape(2, energy_count, block_count, devices, row_count, orbitals)
    outgoing = jnp.transpose(outgoing, (3, 1, 0, 2, 4, 5))
    rows = lax.all_to_all(outgoing, "energy", split_axis=0, concat_axis=0, tiled=True)
    rows = rows.reshape(devices * energy_count, 2, block_count, row_count, orbitals)
    lesser_rows = rows[:, 0]
    greater_rows = rows[:, 1]
    less_sum = jnp.zeros(lesser_rows.shape, jnp.float32)
    great_sum = jnp.zeros(greater_rows.shape, jnp.float32)
    for branch in range(2):
        offset = phonon_shift[branch]
        less_sum = (
            less_sum
            + (1.0 + occupied) * displaced(lesser_rows, offset)
            + occupied * displaced(lesser_rows, -offset)
        )
        great_sum = (
            great_sum
            + (1.0 + occupied) * displaced(greater_rows, -offset)
            + occupied * displaced(greater_rows, offset)
        )
    sigma_l = (phonon_coupling * less_sum).astype(jnp.bfloat16)
    sigma_g = (phonon_coupling * great_sum).astype(jnp.bfloat16)
    scattering = jnp.sum(
        sigma_l.astype(jnp.float32) * greater_rows.astype(jnp.float32)
        - sigma_g.astype(jnp.float32) * lesser_rows.astype(jnp.float32),
        axis=(2, 3),
    )
    parts = scattering.reshape(devices, energy_count, block_count)
    parts = lax.all_to_all(parts, "energy", split_axis=0, concat_axis=0, tiled=True)
    current = jnp.sum(parts, axis=0) / orbitals
    return (sigma_l, sigma_g, current, density)


def solution(mesh):
    return jax.shard_map(
        local,
        mesh=mesh,
        in_specs=(
            P("energy", "space", None, None),
            P("energy", "space", None, None),
            P("energy", "space", None, None),
            P("space", None, None),
            P("energy", None),
            P(),
            P(),
        ),
        out_specs=(
            P(None, "space", "energy", None),
            P(None, "space", "energy", None),
            P("energy", "space"),
            P("energy", "space"),
        ),
        check_vma=False,
    )
```

```python
import functools

import jax
import jax.numpy as jnp
from jax import lax
from jax.experimental import pallas as pl
from jax.experimental.pallas import tpu as pltpu
from jax.sharding import PartitionSpec as P

phonon_occupation = 0.5

VMEM = pl.BlockSpec(memory_space=pltpu.VMEM)
SMEM = pl.BlockSpec(memory_space=pltpu.SMEM)
ANY = pl.BlockSpec(memory_space=pl.ANY)


def shifted(value, axis, steps):
    count = lax.axis_size(axis)
    initial, last = (max(0, -steps), min(count, count - steps))
    return lax.ppermute(value, axis, [(source, source + steps) for source in range(initial, last)])


def params():
    return pltpu.CompilerParams(vmem_limit_bytes=24 * 1024 * 1024)


def product(left, right):
    return jnp.dot(left, right, preferred_element_type=jnp.float32)


def product_t(left, right):
    return lax.dot_general(
        left, right, (((1,), (1,)), ((), ())), preferred_element_type=jnp.float32
    )


def pack_kernel(block_of, green, less, great, coupling, packed, sems):
    block = block_of()
    copies = [
        pltpu.make_async_copy(ref, packed.at[slot], sems.at[slot])
        for slot, ref in enumerate(
            (green.at[0, block], less.at[0, block], great.at[0, block], coupling.at[block])
        )
    ]
    for copy in copies:
        copy.start()
    for copy in copies:
        copy.wait()


def pack(block_of, green, less, great, coupling):
    orbitals = green.shape[-1]
    return pl.pallas_call(
        functools.partial(pack_kernel, block_of),
        out_shape=jax.ShapeDtypeStruct((4, orbitals, orbitals), green.dtype),
        in_specs=[ANY] * 4,
        out_specs=ANY,
        scratch_shapes=[pltpu.SemaphoreType.DMA((4,))],
        compiler_params=params(),
    )(green, less, great, coupling)


def through(operator, less, great):
    rows = operator.shape[0]
    half = product(operator, jnp.concatenate([less, great], 1)).astype(jnp.bfloat16)
    stacked = jnp.concatenate([half[:, :rows], half[:, rows:]], 0)
    return product_t(stacked, operator)


def green_kernel(swap, split, active, green, less, great, coupling, *rest):
    halos, (outgoing, diagonal, source) = rest[:-3], rest[-3:]
    block_count, orbitals = green.shape[1], green.shape[2]
    energy, place = lax.axis_index("energy"), lax.axis_index("space")
    places = lax.axis_size("space")
    open_count = active[energy] - place * block_count
    for block in range(block_count):
        source[block] = jnp.concatenate([less[0, block], great[0, block]], 0).astype(jnp.float32)
    for block in range(block_count):
        retarded, low, high = green[0, block], less[0, block], great[0, block]
        rise = block + 1 < block_count
        fall = block > 0
        hops = []
        if rise:
            hops.append(coupling[block].T)
        if fall:
            hops.append(coupling[block - 1])
        hops = product(jnp.concatenate(hops, 0), retarded).astype(jnp.bfloat16)
        both = product(hops, jnp.concatenate([low, high], 1)).astype(jnp.bfloat16)
        first = 0
        for wanted, target in ((rise, block + 1), (fall, block - 1)):
            if wanted:
                piece = slice(first, first + orbitals)
                stacked = jnp.concatenate([both[piece, :orbitals], both[piece, orbitals:]], 0)
                source[target] = source[target] + product_t(stacked, hops[piece])
                first += orbitals
    last = block_count - 1
    if swap:
        (halo,) = halos
        hop = jnp.where(place == 0, coupling[last], halo[3].T)
        edge = through(product(hop, halo[0]).astype(jnp.bfloat16), halo[1], halo[2])
        source[0] = source[0] + jnp.where(place > 0, edge, 0.0)
        source[last] = source[last] + jnp.where(place == 0, edge, 0.0)
    elif halos:
        before, after = halos
        hop = product(before[3].T, before[0]).astype(jnp.bfloat16)
        source[0] = source[0] + through(hop, before[1], before[2])
        hop = product(coupling[last], after[0]).astype(jnp.bfloat16)
        source[last] = source[last] + through(hop, after[1], after[2])
    row_ids = lax.broadcasted_iota(jnp.int32, (orbitals, orbitals), 0)
    column_ids = lax.broadcasted_iota(jnp.int32, (orbitals, orbitals), 1)
    on_diagonal = row_ids == column_ids
    for block in range(block_count):
        retarded = green[0, block]
        middle = source[block].astype(jnp.bfloat16)
        half = product(retarded, jnp.concatenate([middle[:orbitals], middle[orbitals:]], 1))
        half = half.astype(jnp.bfloat16)
        stacked = jnp.concatenate([half[:, :orbitals], half[:, orbitals:]], 0)
        result = product_t(stacked, retarded)
        result = result * (block < open_count).astype(jnp.float32)
        kinds = [result[:orbitals], result[orbitals:]]
        rounded = [kind.astype(jnp.bfloat16) for kind in kinds]
        total = rounded[0].astype(jnp.float32) + rounded[1].astype(jnp.float32)
        diagonal[block : block + 1] = jnp.sum(
            jnp.where(on_diagonal, total, 0.0), axis=0, keepdims=True
        )
        for kind in range(2):
            if split:
                devices, _, _, rows, _ = outgoing.shape
                outgoing[:, kind, block] = (
                    kinds[kind].reshape(devices, rows, orbitals).astype(jnp.bfloat16)
                )
            else:
                outgoing[kind, block] = rounded[kind]


def current_kernel(shift, rows, strength, parts, total):
    energies, _, block_count, row_count, orbitals = rows.shape
    total[...] = jnp.zeros_like(total)
    scale = strength[...] * (1.0 / orbitals)

    def step(energy, carry):
        low = rows[energy, 0].astype(jnp.float32) * scale
        high = rows[energy, 1].astype(jnp.float32) * scale
        for branch in range(2):
            target = energy + shift[branch]
            inside = (target < energies).astype(jnp.float32)
            there = jnp.minimum(target, energies - 1)
            gain = (1.0 + phonon_occupation) * inside
            loss = phonon_occupation * inside
            pair = gain * (high * rows[there, 0].astype(jnp.float32)) - loss * (
                low * rows[there, 1].astype(jnp.float32)
            )
            total[energy] = total[energy] + pair
            total[there] = total[there] - pair
        return carry

    lax.fori_loop(0, energies, step, 0)
    summed = jnp.sum(total[...], axis=2).reshape(energies * block_count, orbitals)
    ones = jnp.ones((8, orbitals), jnp.float32)
    flat = lax.dot_general(
        ones,
        summed,
        (((1,), (1,)), ((), ())),
        precision=lax.Precision.HIGHEST,
        preferred_element_type=jnp.float32,
    )
    for energy in range(energies):
        parts[energy] = flat[0:1, energy * block_count : (energy + 1) * block_count]


def sigma_kernel(shift, rows, strength, less_out, great_out):
    energies = rows.shape[0]
    factor = strength[...]

    def step(energy, carry):
        less_sum, great_sum = 0.0, 0.0
        for branch in range(2):
            above, below = energy + shift[branch], energy - shift[branch]
            has_above = (above < energies).astype(jnp.float32)
            has_below = (below >= 0).astype(jnp.float32)
            above = jnp.minimum(above, energies - 1)
            below = jnp.maximum(below, 0)
            more, fewer = 1.0 + phonon_occupation, phonon_occupation
            less_sum = (
                less_sum
                + (more * has_above) * rows[above, 0].astype(jnp.float32)
                + (fewer * has_below) * rows[below, 0].astype(jnp.float32)
            )
            great_sum = (
                great_sum
                + (more * has_below) * rows[below, 1].astype(jnp.float32)
                + (fewer * has_above) * rows[above, 1].astype(jnp.float32)
            )
        less_out[energy] = (factor * less_sum).astype(less_out.dtype)
        great_out[energy] = (factor * great_sum).astype(great_out.dtype)
        return carry

    lax.fori_loop(0, energies, step, 0)


def local(
    green_ret, prior_less, prior_great, coupling, phonon_coupling, phonon_shift, active_blocks
):
    _, block_count, orbitals, _ = green_ret.shape
    devices, places = lax.axis_size("energy"), lax.axis_size("space")
    row_count = orbitals // devices
    arrays = (green_ret, prior_less, prior_great, coupling)
    last = block_count - 1
    swap = places == 2
    if swap:
        edge = pack(lambda: last * (1 - lax.axis_index("space")), *arrays)
        halos = (lax.ppermute(edge, "space", [(0, 1), (1, 0)]),)
    elif places > 1:
        halos = (
            shifted(pack(lambda: last, *arrays), "space", 1),
            shifted(pack(lambda: 0, *arrays), "space", -1),
        )
    else:
        halos = ()
    split = row_count % 8 == 0
    if split:
        out_shape = (devices, 2, block_count, row_count, orbitals)
    else:
        out_shape = (2, block_count, orbitals, orbitals)
    outgoing, diagonal = pl.pallas_call(
        functools.partial(green_kernel, swap, split),
        out_shape=(
            jax.ShapeDtypeStruct(out_shape, jnp.bfloat16),
            jax.ShapeDtypeStruct((block_count, orbitals), jnp.float32),
        ),
        in_specs=[SMEM] + [VMEM] * (4 + len(halos)),
        out_specs=(VMEM, VMEM),
        scratch_shapes=[pltpu.VMEM((block_count, 2 * orbitals, orbitals), jnp.float32)],
        compiler_params=params(),
    )(active_blocks, *arrays, *halos)
    if not split:
        outgoing = outgoing.reshape(2, block_count, devices, row_count, orbitals)
        outgoing = jnp.transpose(outgoing, (2, 0, 1, 3, 4))
    ldos = jnp.sum(diagonal, axis=1)[None, :] / orbitals
    rows = lax.all_to_all(outgoing, "energy", split_axis=0, concat_axis=0, tiled=True)
    parts = pl.pallas_call(
        current_kernel,
        out_shape=jax.ShapeDtypeStruct((devices, 1, block_count), jnp.float32),
        in_specs=[SMEM, VMEM, VMEM],
        out_specs=VMEM,
        scratch_shapes=[pltpu.VMEM((devices, block_count, row_count, orbitals), jnp.float32)],
        compiler_params=params(),
    )(phonon_shift, rows, phonon_coupling)
    parts = lax.all_to_all(parts, "energy", split_axis=0, concat_axis=0, tiled=True)
    out = jax.ShapeDtypeStruct((devices, block_count, row_count, orbitals), jnp.bfloat16)
    sigma_l, sigma_g = pl.pallas_call(
        sigma_kernel,
        out_shape=(out, out),
        in_specs=[SMEM, VMEM, VMEM],
        out_specs=(VMEM, VMEM),
        compiler_params=params(),
        cost_estimate=pl.CostEstimate(
            flops=20 * rows.size, bytes_accessed=4 * rows.size, transcendentals=0
        ),
    )(phonon_shift, rows, phonon_coupling)
    current = jnp.sum(parts, axis=0)
    return (sigma_l, sigma_g, current, ldos)


def solution(mesh):
    return jax.shard_map(
        local,
        mesh=mesh,
        in_specs=(
            P("energy", "space", None, None),
            P("energy", "space", None, None),
            P("energy", "space", None, None),
            P("space", None, None),
            P("energy", None),
            P(),
            P(),
        ),
        out_specs=(
            P(None, "space", "energy", None),
            P(None, "space", "energy", None),
            P("energy", "space"),
            P("energy", "space"),
        ),
        check_vma=False,
    )
```

```python
import functools

import jax
import jax.numpy as jnp
from jax import lax
from jax.experimental import pallas as pl
from jax.experimental.pallas import tpu as pltpu
from jax.sharding import PartitionSpec as P

phonon_occupation = 0.5

VMEM = pl.BlockSpec(memory_space=pltpu.VMEM)
SMEM = pl.BlockSpec(memory_space=pltpu.SMEM)
ANY = pl.BlockSpec(memory_space=pl.ANY)


def shifted(value, axis, steps):
    count = lax.axis_size(axis)
    initial, last = (max(0, -steps), min(count, count - steps))
    return lax.ppermute(value, axis, [(source, source + steps) for source in range(initial, last)])


def params():
    return pltpu.CompilerParams(vmem_limit_bytes=24 * 1024 * 1024)


def product(left, right):
    return jnp.dot(left, right, preferred_element_type=jnp.float32)


def product_t(left, right):
    return lax.dot_general(
        left, right, (((1,), (1,)), ((), ())), preferred_element_type=jnp.float32
    )


def held(shape, dtype):
    return pltpu.VMEM(shape, dtype)


def in_hbm(*arrays):
    return [pltpu.with_memory_space_constraint(array, pltpu.HBM) for array in arrays]


def pack_kernel(block_of, green, less, great, coupling, packed, sems):
    block = block_of()
    copies = [
        pltpu.make_async_copy(ref, packed.at[slot], sems.at[slot])
        for slot, ref in enumerate(
            (green.at[0, block], less.at[0, block], great.at[0, block], coupling.at[block])
        )
    ]
    for copy in copies:
        copy.start()
    for copy in copies:
        copy.wait()


def pack(block_of, green, less, great, coupling):
    orbitals = green.shape[-1]
    return pl.pallas_call(
        functools.partial(pack_kernel, block_of),
        out_shape=held((4, orbitals, orbitals), green.dtype),
        in_specs=[ANY] * 4,
        out_specs=VMEM,
        scratch_shapes=[pltpu.SemaphoreType.DMA((4,))],
        compiler_params=params(),
    )(*in_hbm(green, less, great, coupling))


def through(operator, less, great):
    rows = operator.shape[0]
    half = product(operator, jnp.concatenate([less, great], 1)).astype(jnp.bfloat16)
    stacked = jnp.concatenate([half[:, :rows], half[:, rows:]], 0)
    return product_t(stacked, operator)


def hop_kernel(
    green_in, less_in, great_in, coupling_in, green, coupling, source, less, great, sems
):
    block_count, orbitals = green.shape[0], green.shape[1]
    copies = []
    for block in range(block_count):
        pairs = (
            (coupling_in.at[block], coupling.at[block]),
            (green_in.at[0, block], green.at[block]),
            (less_in.at[0, block], less.at[block]),
            (great_in.at[0, block], great.at[block]),
        )
        copies.append(
            [
                pltpu.make_async_copy(origin, target, sems.at[block, slot])
                for slot, (origin, target) in enumerate(pairs)
            ]
        )
    for group in copies:
        for copy in group:
            copy.start()
    for block in range(block_count):
        for copy in copies[block]:
            copy.wait()
        retarded, low, high = green[block], less[block], great[block]
        rise = block + 1 < block_count
        fall = block > 0
        hops = []
        if rise:
            hops.append(coupling[block].T)
        if fall:
            hops.append(coupling[block - 1])
        hops = product(jnp.concatenate(hops, 0), retarded).astype(jnp.bfloat16)
        both = product(hops, jnp.concatenate([low, high], 1)).astype(jnp.bfloat16)
        prior = jnp.concatenate([low, high], 0).astype(jnp.float32)
        source[block] = source[block] + prior if fall else prior
        first = 0
        for wanted, target in ((rise, block + 1), (fall, block - 1)):
            if wanted:
                piece = slice(first, first + orbitals)
                stacked = jnp.concatenate([both[piece, :orbitals], both[piece, orbitals:]], 0)
                moved = product_t(stacked, hops[piece])
                source[target] = moved if target > block else source[target] + moved
                first += orbitals


def green_kernel(swap, split, active, green, coupling, source, *rest):
    halos, (outgoing, diagonal) = rest[:-2], rest[-2:]
    block_count, orbitals = green.shape[0], green.shape[1]
    energy, place = lax.axis_index("energy"), lax.axis_index("space")
    open_count = active[energy] - place * block_count
    last = block_count - 1
    added = {}
    if swap:
        (halo,) = halos
        hop = jnp.where(place == 0, coupling[last], halo[3].T)
        edge = through(product(hop, halo[0]).astype(jnp.bfloat16), halo[1], halo[2])
        added = {0: jnp.where(place > 0, edge, 0.0), last: jnp.where(place == 0, edge, 0.0)}
    elif halos:
        before, after = halos
        hop = product(before[3].T, before[0]).astype(jnp.bfloat16)
        added[0] = through(hop, before[1], before[2])
        hop = product(coupling[last], after[0]).astype(jnp.bfloat16)
        added[last] = through(hop, after[1], after[2])
    row_ids = lax.broadcasted_iota(jnp.int32, (orbitals, orbitals), 0)
    column_ids = lax.broadcasted_iota(jnp.int32, (orbitals, orbitals), 1)
    on_diagonal = row_ids == column_ids
    for block in [*range(1, last), 0, last]:
        retarded, middle = green[block], source[block]
        if block in added:
            middle = middle + added[block]
        middle = middle.astype(jnp.bfloat16)
        half = product(retarded, jnp.concatenate([middle[:orbitals], middle[orbitals:]], 1))
        half = half.astype(jnp.bfloat16)
        stacked = jnp.concatenate([half[:, :orbitals], half[:, orbitals:]], 0)
        result = product_t(stacked, retarded)
        result = result * (block < open_count).astype(jnp.float32)
        kinds = [result[:orbitals], result[orbitals:]]
        rounded = [kind.astype(jnp.bfloat16) for kind in kinds]
        total = rounded[0].astype(jnp.float32) + rounded[1].astype(jnp.float32)
        diagonal[block : block + 1] = jnp.sum(
            jnp.where(on_diagonal, total, 0.0), axis=0, keepdims=True
        )
        for kind in range(2):
            if split:
                devices, _, _, rows, _ = outgoing.shape
                outgoing[:, kind, block] = (
                    kinds[kind].reshape(devices, rows, orbitals).astype(jnp.bfloat16)
                )
            else:
                outgoing[kind, block] = rounded[kind]


def current_kernel(shift, rows, strength, parts, total):
    energies, _, block_count, row_count, orbitals = rows.shape
    total[...] = jnp.zeros_like(total)
    scale = strength[...] * (1.0 / orbitals)

    def step(energy, carry):
        low = rows[energy, 0].astype(jnp.float32) * scale
        high = rows[energy, 1].astype(jnp.float32) * scale
        for branch in range(2):
            target = energy + shift[branch]
            inside = (target < energies).astype(jnp.float32)
            there = jnp.minimum(target, energies - 1)
            gain = (1.0 + phonon_occupation) * inside
            loss = phonon_occupation * inside
            pair = gain * (high * rows[there, 0].astype(jnp.float32)) - loss * (
                low * rows[there, 1].astype(jnp.float32)
            )
            total[energy] = total[energy] + pair
            total[there] = total[there] - pair
        return carry

    lax.fori_loop(0, energies, step, 0)
    summed = jnp.sum(total[...], axis=2).reshape(energies * block_count, orbitals)
    ones = jnp.ones((8, orbitals), jnp.float32)
    flat = lax.dot_general(
        ones,
        summed,
        (((1,), (1,)), ((), ())),
        precision=lax.Precision.HIGHEST,
        preferred_element_type=jnp.float32,
    )
    for energy in range(energies):
        parts[energy] = flat[0:1, energy * block_count : (energy + 1) * block_count]


def sigma_kernel(shift, rows, strength, less_out, great_out):
    energies = rows.shape[0]
    factor = strength[...]

    def step(energy, carry):
        less_sum, great_sum = 0.0, 0.0
        for branch in range(2):
            above, below = energy + shift[branch], energy - shift[branch]
            has_above = (above < energies).astype(jnp.float32)
            has_below = (below >= 0).astype(jnp.float32)
            above = jnp.minimum(above, energies - 1)
            below = jnp.maximum(below, 0)
            more, fewer = 1.0 + phonon_occupation, phonon_occupation
            less_sum = (
                less_sum
                + (more * has_above) * rows[above, 0].astype(jnp.float32)
                + (fewer * has_below) * rows[below, 0].astype(jnp.float32)
            )
            great_sum = (
                great_sum
                + (more * has_below) * rows[below, 1].astype(jnp.float32)
                + (fewer * has_above) * rows[above, 1].astype(jnp.float32)
            )
        less_out[energy] = (factor * less_sum).astype(less_out.dtype)
        great_out[energy] = (factor * great_sum).astype(great_out.dtype)
        return carry

    lax.fori_loop(0, energies, step, 0)


def local(
    green_ret, prior_less, prior_great, coupling, phonon_coupling, phonon_shift, active_blocks
):
    _, block_count, orbitals, _ = green_ret.shape
    devices, places = lax.axis_size("energy"), lax.axis_size("space")
    row_count = orbitals // devices
    arrays = (green_ret, prior_less, prior_great, coupling)
    last = block_count - 1
    swap = places == 2
    if swap:
        edge = pack(lambda: last * (1 - lax.axis_index("space")), *arrays)
        halos = (lax.ppermute(edge, "space", [(0, 1), (1, 0)]),)
    elif places > 1:
        halos = (
            shifted(pack(lambda: last, *arrays), "space", 1),
            shifted(pack(lambda: 0, *arrays), "space", -1),
        )
    else:
        halos = ()
    split = row_count % 8 == 0
    if split:
        out_shape = (devices, 2, block_count, row_count, orbitals)
    else:
        out_shape = (2, block_count, orbitals, orbitals)
    blocks = (block_count, orbitals, orbitals)
    green, hops, source = pl.pallas_call(
        hop_kernel,
        out_shape=(
            held(blocks, jnp.bfloat16),
            held(blocks, jnp.bfloat16),
            held((block_count, 2 * orbitals, orbitals), jnp.float32),
        ),
        in_specs=[ANY] * 4,
        out_specs=(VMEM, VMEM, VMEM),
        scratch_shapes=[
            pltpu.VMEM(blocks, jnp.bfloat16),
            pltpu.VMEM(blocks, jnp.bfloat16),
            pltpu.SemaphoreType.DMA((block_count, 4)),
        ],
        compiler_params=params(),
        cost_estimate=pl.CostEstimate(
            flops=20 * block_count * orbitals**3,
            bytes_accessed=8 * block_count * orbitals**2,
            transcendentals=0,
        ),
    )(*in_hbm(*arrays))
    outgoing, diagonal = pl.pallas_call(
        functools.partial(green_kernel, swap, split),
        out_shape=(
            held(out_shape, jnp.bfloat16),
            jax.ShapeDtypeStruct((block_count, orbitals), jnp.float32),
        ),
        in_specs=[SMEM] + [VMEM] * (3 + len(halos)),
        out_specs=(VMEM, VMEM),
        compiler_params=params(),
    )(active_blocks, green, hops, source, *halos)
    if not split:
        outgoing = outgoing.reshape(2, block_count, devices, row_count, orbitals)
        outgoing = jnp.transpose(outgoing, (2, 0, 1, 3, 4))
    ldos = jnp.sum(diagonal, axis=1)[None, :] / orbitals
    rows = lax.all_to_all(outgoing, "energy", split_axis=0, concat_axis=0, tiled=True)
    parts = pl.pallas_call(
        current_kernel,
        out_shape=held((devices, 1, block_count), jnp.float32),
        in_specs=[SMEM, VMEM, VMEM],
        out_specs=VMEM,
        scratch_shapes=[pltpu.VMEM((devices, block_count, row_count, orbitals), jnp.float32)],
        compiler_params=params(),
    )(phonon_shift, rows, phonon_coupling)
    parts = lax.all_to_all(parts, "energy", split_axis=0, concat_axis=0, tiled=True)
    out = jax.ShapeDtypeStruct((devices, block_count, row_count, orbitals), jnp.bfloat16)
    sigma_l, sigma_g = pl.pallas_call(
        sigma_kernel,
        out_shape=(out, out),
        in_specs=[SMEM, VMEM, VMEM],
        out_specs=(VMEM, VMEM),
        compiler_params=params(),
        cost_estimate=pl.CostEstimate(
            flops=20 * rows.size, bytes_accessed=4 * rows.size, transcendentals=0
        ),
    )(phonon_shift, rows, phonon_coupling)
    current = jnp.sum(parts, axis=0)
    return (sigma_l, sigma_g, current, ldos)


def solution(mesh):
    return jax.shard_map(
        local,
        mesh=mesh,
        in_specs=(
            P("energy", "space", None, None),
            P("energy", "space", None, None),
            P("energy", "space", None, None),
            P("space", None, None),
            P("energy", None),
            P(),
            P(),
        ),
        out_specs=(
            P(None, "space", "energy", None),
            P(None, "space", "energy", None),
            P("energy", "space"),
            P("energy", "space"),
        ),
        check_vma=False,
    )
```

```python
import functools

import jax
import jax.numpy as jnp
from jax import lax
from jax.experimental import pallas as pl
from jax.experimental.pallas import tpu as pltpu
from jax.sharding import PartitionSpec as P

phonon_occupation = 0.5

VMEM = pl.BlockSpec(memory_space=pltpu.VMEM)
SMEM = pl.BlockSpec(memory_space=pltpu.SMEM)
ANY = pl.BlockSpec(memory_space=pl.ANY)


def shifted(value, axis, steps):
    count = lax.axis_size(axis)
    initial, last = (max(0, -steps), min(count, count - steps))
    return lax.ppermute(value, axis, [(source, source + steps) for source in range(initial, last)])


def params():
    return pltpu.CompilerParams(vmem_limit_bytes=24 * 1024 * 1024)


def product(left, right):
    return jnp.dot(left, right, preferred_element_type=jnp.float32)


def product_t(left, right):
    return lax.dot_general(
        left, right, (((1,), (1,)), ((), ())), preferred_element_type=jnp.float32
    )


def held(shape, dtype):
    return pltpu.VMEM(shape, dtype)


def in_hbm(*arrays):
    return [pltpu.with_memory_space_constraint(array, pltpu.HBM) for array in arrays]


def in_smem(array):
    return pltpu.with_memory_space_constraint(array, pltpu.SMEM)


def load_kernel(edges, *refs):
    inputs, active, shift = refs[:4], refs[4], refs[5]
    outputs, steps, open_mask = refs[6:10], refs[10], refs[11]
    packed, counts, sems = refs[12 : 12 + len(edges)], refs[-2], refs[-1]
    blocks = [ref if ref.ndim == 3 else ref.at[0] for ref in inputs]
    pairs = [(active, counts), (shift, steps)]
    for block_of, target in zip(edges, packed):
        block = block_of()
        pairs += [(ref.at[block], target.at[slot]) for slot, ref in enumerate(blocks)]
    pairs += list(zip(blocks, outputs))
    copies = [
        pltpu.make_async_copy(origin, target, sems.at[index])
        for index, (origin, target) in enumerate(pairs)
    ]
    for copy in copies:
        copy.start()
    for copy in copies:
        copy.wait()
    block_count = open_mask.shape[0]
    open_count = counts[lax.axis_index("energy")] - lax.axis_index("space") * block_count
    block_ids = lax.broadcasted_iota(jnp.int32, open_mask.shape, 0)
    open_mask[...] = (block_ids < open_count).astype(jnp.float32)


def load(edges, arrays, active, shift):
    _, block_count, orbitals, _ = arrays[0].shape
    blocks = held((block_count, orbitals, orbitals), jnp.bfloat16)
    edge = held((len(arrays), orbitals, orbitals), jnp.bfloat16)
    copies = len(arrays) * (1 + len(edges)) + 2
    results = pl.pallas_call(
        functools.partial(load_kernel, edges),
        out_shape=(
            *[blocks] * len(arrays),
            pltpu.SMEM(shift.shape, shift.dtype),
            held((block_count, orbitals), jnp.float32),
            *[edge] * len(edges),
        ),
        in_specs=[ANY] * (len(arrays) + 2),
        out_specs=(*[VMEM] * len(arrays), SMEM, VMEM, *[VMEM] * len(edges)),
        scratch_shapes=[
            pltpu.SMEM(active.shape, active.dtype),
            pltpu.SemaphoreType.DMA((copies,)),
        ],
        compiler_params=params(),
    )(*in_hbm(*arrays, active, shift))
    kept = len(arrays)
    return results[:kept], results[kept], results[kept + 1], results[kept + 2 :]


def through(operator, less, great):
    rows = operator.shape[0]
    half = product(operator, jnp.concatenate([less, great], 1)).astype(jnp.bfloat16)
    stacked = jnp.concatenate([half[:, :rows], half[:, rows:]], 0)
    return product_t(stacked, operator)


def hop_kernel(green, less, great, coupling, source):
    block_count, orbitals = green.shape[0], green.shape[1]
    blocks = range(block_count)
    hops, both = [], []
    for block in blocks:
        factors = []
        if block + 1 < block_count:
            factors.append(coupling[block].T)
        if block > 0:
            factors.append(coupling[block - 1])
        hops.append(product(jnp.concatenate(factors, 0), green[block]).astype(jnp.bfloat16))
    for block in blocks:
        prior = jnp.concatenate([less[block], great[block]], 1)
        both.append(product(hops[block], prior).astype(jnp.bfloat16))
    for block in blocks:
        prior = jnp.concatenate([less[block], great[block]], 0).astype(jnp.float32)
        source[block] = source[block] + prior if block > 0 else prior
        first = 0
        for target in (block + 1, block - 1):
            if 0 <= target < block_count:
                piece = slice(first, first + orbitals)
                half = both[block][piece]
                stacked = jnp.concatenate([half[:, :orbitals], half[:, orbitals:]], 0)
                moved = product_t(stacked, hops[block][piece])
                source[target] = moved if target > block else source[target] + moved
                first += orbitals


def green_kernel(swap, split, green, coupling, source, open_mask, *rest):
    halos, (outgoing, diagonal) = rest[:-2], rest[-2:]
    block_count, orbitals = green.shape[0], green.shape[1]
    place = lax.axis_index("space")
    last = block_count - 1
    added = {}
    if swap:
        (halo,) = halos
        hop = jnp.where(place == 0, coupling[last], halo[3].T)
        edge = through(product(hop, halo[0]).astype(jnp.bfloat16), halo[1], halo[2])
        added = {0: jnp.where(place > 0, edge, 0.0), last: jnp.where(place == 0, edge, 0.0)}
    elif halos:
        before, after = halos
        hop = product(before[3].T, before[0]).astype(jnp.bfloat16)
        added[0] = through(hop, before[1], before[2])
        hop = product(coupling[last], after[0]).astype(jnp.bfloat16)
        added[last] = through(hop, after[1], after[2])
    row_ids = lax.broadcasted_iota(jnp.int32, (orbitals, orbitals), 0)
    column_ids = lax.broadcasted_iota(jnp.int32, (orbitals, orbitals), 1)
    on_diagonal = row_ids == column_ids
    order = [*range(1, last), 0, last]
    halves, kinds = {}, {}
    for block in order:
        middle = source[block]
        if block in added:
            middle = middle + added[block]
        middle = middle.astype(jnp.bfloat16)
        middle = jnp.concatenate([middle[:orbitals], middle[orbitals:]], 1)
        halves[block] = product(green[block], middle).astype(jnp.bfloat16)
    for block in order:
        half = halves[block]
        stacked = jnp.concatenate([half[:, :orbitals], half[:, orbitals:]], 0)
        result = product_t(stacked, green[block]) * open_mask[block : block + 1]
        kinds[block] = [result[:orbitals], result[orbitals:]]
        total = sum(kind.astype(jnp.bfloat16).astype(jnp.float32) for kind in kinds[block])
        diagonal[block : block + 1] = jnp.sum(
            jnp.where(on_diagonal, total, 0.0), axis=0, keepdims=True
        )
        if not split:
            for kind in range(2):
                outgoing[kind, block] = kinds[block][kind].astype(jnp.bfloat16)
    if split:
        devices, _, rows, _ = outgoing.shape
        rows //= block_count
        for block in range(0, block_count, 2):
            for kind in range(2):
                pair = [
                    kinds[block + step][kind].reshape(devices, rows, orbitals) for step in range(2)
                ]
                outgoing[:, kind, block * rows : (block + 2) * rows] = jnp.concatenate(
                    pair, 1
                ).astype(jnp.bfloat16)


def spread(strength, rows):
    return jnp.concatenate([strength] * (rows // strength.shape[0]), 0)


def current_kernel(shift, rows, strength, parts, wide, total):
    energies, _, row_count, orbitals = rows.shape
    block_count = total.shape[1]
    pad = energies // 2
    edge = jnp.zeros((pad, 2, row_count, orbitals), jnp.float32)
    wide[0:pad] = edge
    wide[pad + energies :] = edge
    wide[pad : pad + energies] = rows[...].astype(jnp.float32)
    scale = spread(strength[...] * (1.0 / orbitals), row_count)
    first, second = shift[0], shift[1]

    def step(energy, carry):
        here = energy + pad
        above, below = (
            [wide[here + first, kind] + wide[here + second, kind] for kind in range(2)],
            [wide[here - first, kind] + wide[here - second, kind] for kind in range(2)],
        )
        gain = (1.0 + phonon_occupation) * above[0] + phonon_occupation * below[0]
        loss = (1.0 + phonon_occupation) * below[1] + phonon_occupation * above[1]
        flow = (gain * wide[here, 1] - loss * wide[here, 0]) * scale
        total[energy] = jnp.sum(flow.reshape(block_count, -1, orbitals), axis=1)
        return carry

    lax.fori_loop(0, energies, step, 0, unroll=4)
    summed = total[...].reshape(energies * block_count, orbitals)
    coarse = summed.astype(jnp.bfloat16)
    fine = (summed - coarse.astype(jnp.float32)).astype(jnp.bfloat16)
    ones = jnp.ones((8, 2 * orbitals), jnp.bfloat16)
    flat = product_t(ones, jnp.concatenate([coarse, fine], 1))
    for energy in range(energies):
        parts[energy] = flat[0:1, energy * block_count : (energy + 1) * block_count]


def sigma_kernel(shift, rows, strength, less_out, great_out):
    energies = rows.shape[0]
    factor = spread(strength[...], rows.shape[2])

    def step(energy, carry):
        less_sum, great_sum = 0.0, 0.0
        for branch in range(2):
            above, below = energy + shift[branch], energy - shift[branch]
            has_above = (above < energies).astype(jnp.float32)
            has_below = (below >= 0).astype(jnp.float32)
            above = jnp.minimum(above, energies - 1)
            below = jnp.maximum(below, 0)
            more, fewer = 1.0 + phonon_occupation, phonon_occupation
            less_sum = (
                less_sum
                + (more * has_above) * rows[above, 0].astype(jnp.float32)
                + (fewer * has_below) * rows[below, 0].astype(jnp.float32)
            )
            great_sum = (
                great_sum
                + (more * has_below) * rows[below, 1].astype(jnp.float32)
                + (fewer * has_above) * rows[above, 1].astype(jnp.float32)
            )
        less_out[energy] = (factor * less_sum).astype(less_out.dtype)
        great_out[energy] = (factor * great_sum).astype(great_out.dtype)
        return carry

    lax.fori_loop(0, energies, step, 0)


def local(
    green_ret, prior_less, prior_great, coupling, phonon_coupling, phonon_shift, active_blocks
):
    _, block_count, orbitals, _ = green_ret.shape
    devices, places = lax.axis_size("energy"), lax.axis_size("space")
    row_count = orbitals // devices
    last = block_count - 1
    swap = places == 2
    if swap:
        edges = [lambda: last * (1 - lax.axis_index("space"))]
    elif places > 1:
        edges = [lambda: last, lambda: 0]
    else:
        edges = []
    arrays, shift, open_mask, packed = load(
        edges, (green_ret, prior_less, prior_great, coupling), active_blocks, phonon_shift
    )
    green, less, great, coupling = arrays
    if swap:
        halos = (lax.ppermute(packed[0], "space", [(0, 1), (1, 0)]),)
    else:
        halos = tuple(
            shifted(edge, "space", step) for edge, step in zip(packed, (1, -1), strict=False)
        )
    source = pl.pallas_call(
        hop_kernel,
        out_shape=held((block_count, 2 * orbitals, orbitals), jnp.float32),
        in_specs=[VMEM] * 4,
        out_specs=VMEM,
        compiler_params=params(),
        cost_estimate=pl.CostEstimate(
            flops=20 * block_count * orbitals**3,
            bytes_accessed=8 * block_count * orbitals**2,
            transcendentals=0,
        ),
    )(green, less, great, coupling)
    split = row_count % 8 == 0 and block_count % 2 == 0
    if split:
        out_shape = (devices, 2, block_count * row_count, orbitals)
    else:
        out_shape = (2, block_count, orbitals, orbitals)
    outgoing, diagonal = pl.pallas_call(
        functools.partial(green_kernel, swap, split),
        out_shape=(
            held(out_shape, jnp.bfloat16),
            jax.ShapeDtypeStruct((block_count, orbitals), jnp.float32),
        ),
        in_specs=[VMEM] * (4 + len(halos)),
        out_specs=(VMEM, VMEM),
        compiler_params=params(),
    )(green, coupling, source, open_mask, *halos)
    if not split:
        outgoing = outgoing.reshape(2, block_count, devices, row_count, orbitals)
        outgoing = jnp.transpose(outgoing, (2, 0, 1, 3, 4))
        outgoing = outgoing.reshape(devices, 2, block_count * row_count, orbitals)
    ldos = jnp.sum(diagonal, axis=1)[None, :] / orbitals
    rows = lax.all_to_all(outgoing, "energy", split_axis=0, concat_axis=0, tiled=True)
    parts = pl.pallas_call(
        current_kernel,
        out_shape=held((devices, 1, block_count), jnp.float32),
        in_specs=[SMEM, VMEM, VMEM],
        out_specs=VMEM,
        scratch_shapes=[
            pltpu.VMEM((2 * devices, *rows.shape[1:]), jnp.float32),
            pltpu.VMEM((devices, block_count, orbitals), jnp.float32),
        ],
        compiler_params=params(),
    )(in_smem(shift), rows, phonon_coupling)
    parts = lax.all_to_all(parts, "energy", split_axis=0, concat_axis=0, tiled=True)
    out = jax.ShapeDtypeStruct((devices, block_count * row_count, orbitals), jnp.bfloat16)
    sigmas = pl.pallas_call(
        sigma_kernel,
        out_shape=(out, out),
        in_specs=[SMEM, VMEM, VMEM],
        out_specs=(VMEM, VMEM),
        compiler_params=params(),
        cost_estimate=pl.CostEstimate(
            flops=20 * rows.size, bytes_accessed=4 * rows.size, transcendentals=0
        ),
    )(in_smem(shift), rows, phonon_coupling)
    sigma_l, sigma_g = [
        sigma.reshape(devices, block_count, row_count, orbitals) for sigma in sigmas
    ]
    current = jnp.sum(parts, axis=0)
    return (sigma_l, sigma_g, current, ldos)


def solution(mesh):
    return jax.shard_map(
        local,
        mesh=mesh,
        in_specs=(
            P("energy", "space", None, None),
            P("energy", "space", None, None),
            P("energy", "space", None, None),
            P("space", None, None),
            P("energy", None),
            P(),
            P(),
        ),
        out_specs=(
            P(None, "space", "energy", None),
            P(None, "space", "energy", None),
            P("energy", "space"),
            P("energy", "space"),
        ),
        check_vma=False,
    )
```

```python
import functools

import jax
import jax.numpy as jnp
from jax import lax
from jax.experimental import pallas as pl
from jax.experimental.pallas import tpu as pltpu
from jax.sharding import PartitionSpec as P

phonon_occupation = 0.5

VMEM = pl.BlockSpec(memory_space=pltpu.VMEM)
SMEM = pl.BlockSpec(memory_space=pltpu.SMEM)
ANY = pl.BlockSpec(memory_space=pl.ANY)


def shifted(value, axis, steps):
    count = lax.axis_size(axis)
    initial, last = (max(0, -steps), min(count, count - steps))
    return lax.ppermute(value, axis, [(source, source + steps) for source in range(initial, last)])


def place_of(index):
    return index // 4, index // 2 % 2, index % 2


def near(count, root):
    def key(index):
        return sum(abs(a - b) for a, b in zip(place_of(root), place_of(index))), index

    return sorted(range(count), key=key)


def orders(count):
    return near(count, 9 * count // 16), near(count, count - 1)


def exchange(chunks, order):
    return lax.all_to_all(
        chunks, "energy", split_axis=0, concat_axis=0, tiled=True, axis_index_groups=[order]
    )


def params():
    return pltpu.CompilerParams(vmem_limit_bytes=24 * 1024 * 1024)


def product(left, right):
    return jnp.dot(left, right, preferred_element_type=jnp.float32)


def product_t(left, right):
    return lax.dot_general(
        left, right, (((1,), (1,)), ((), ())), preferred_element_type=jnp.float32
    )


def held(shape, dtype):
    return pltpu.VMEM(shape, dtype)


def in_hbm(*arrays):
    return [pltpu.with_memory_space_constraint(array, pltpu.HBM) for array in arrays]


def in_smem(array):
    return pltpu.with_memory_space_constraint(array, pltpu.SMEM)


def load_kernel(edges, *refs):
    inputs, active, shift = refs[:4], refs[4], refs[5]
    outputs, steps, open_mask = refs[6:10], refs[10], refs[11]
    packed, counts, sems = refs[12 : 12 + len(edges)], refs[-2], refs[-1]
    blocks = [ref if ref.ndim == 3 else ref.at[0] for ref in inputs]
    pairs = [(active, counts), (shift, steps)]
    for block_of, target in zip(edges, packed):
        block = block_of()
        pairs += [(ref.at[block], target.at[slot]) for slot, ref in enumerate(blocks)]
    pairs += list(zip(blocks, outputs))
    copies = [
        pltpu.make_async_copy(origin, target, sems.at[index])
        for index, (origin, target) in enumerate(pairs)
    ]
    for copy in copies:
        copy.start()
    for copy in copies:
        copy.wait()
    block_count = open_mask.shape[0]
    open_count = counts[lax.axis_index("energy")] - lax.axis_index("space") * block_count
    block_ids = lax.broadcasted_iota(jnp.int32, open_mask.shape, 0)
    open_mask[...] = (block_ids < open_count).astype(jnp.float32)


def load(edges, arrays, active, shift):
    _, block_count, orbitals, _ = arrays[0].shape
    blocks = held((block_count, orbitals, orbitals), jnp.bfloat16)
    edge = held((len(arrays), orbitals, orbitals), jnp.bfloat16)
    copies = len(arrays) * (1 + len(edges)) + 2
    results = pl.pallas_call(
        functools.partial(load_kernel, edges),
        out_shape=(
            *[blocks] * len(arrays),
            pltpu.SMEM(shift.shape, shift.dtype),
            held((block_count, orbitals), jnp.float32),
            *[edge] * len(edges),
        ),
        in_specs=[ANY] * (len(arrays) + 2),
        out_specs=(*[VMEM] * len(arrays), SMEM, VMEM, *[VMEM] * len(edges)),
        scratch_shapes=[
            pltpu.SMEM(active.shape, active.dtype),
            pltpu.SemaphoreType.DMA((copies,)),
        ],
        compiler_params=params(),
    )(*in_hbm(*arrays, active, shift))
    kept = len(arrays)
    return results[:kept], results[kept], results[kept + 1], results[kept + 2 :]


def through(operator, less, great):
    rows = operator.shape[0]
    half = product(operator, jnp.concatenate([less, great], 1)).astype(jnp.bfloat16)
    stacked = jnp.concatenate([half[:, :rows], half[:, rows:]], 0)
    return product_t(stacked, operator)


def hop_kernel(green, less, great, coupling, source):
    block_count, orbitals = green.shape[0], green.shape[1]
    blocks = range(block_count)
    hops, both = [], []
    for block in blocks:
        factors = []
        if block + 1 < block_count:
            factors.append(coupling[block].T)
        if block > 0:
            factors.append(coupling[block - 1])
        hops.append(product(jnp.concatenate(factors, 0), green[block]).astype(jnp.bfloat16))
    for block in blocks:
        prior = jnp.concatenate([less[block], great[block]], 1)
        both.append(product(hops[block], prior).astype(jnp.bfloat16))
    for block in blocks:
        prior = jnp.concatenate([less[block], great[block]], 0).astype(jnp.float32)
        source[block] = source[block] + prior if block > 0 else prior
        first = 0
        for target in (block + 1, block - 1):
            if 0 <= target < block_count:
                piece = slice(first, first + orbitals)
                half = both[block][piece]
                stacked = jnp.concatenate([half[:, :orbitals], half[:, orbitals:]], 0)
                moved = product_t(stacked, hops[block][piece])
                source[target] = moved if target > block else source[target] + moved
                first += orbitals


def green_kernel(swap, split, order, green, coupling, source, open_mask, *rest):
    halos, (outgoing, diagonal) = rest[:-2], rest[-2:]
    block_count, orbitals = green.shape[0], green.shape[1]
    place = lax.axis_index("space")
    last = block_count - 1
    added = {}
    if swap:
        (halo,) = halos
        hop = jnp.where(place == 0, coupling[last], halo[3].T)
        edge = through(product(hop, halo[0]).astype(jnp.bfloat16), halo[1], halo[2])
        added = {0: jnp.where(place > 0, edge, 0.0), last: jnp.where(place == 0, edge, 0.0)}
    elif halos:
        before, after = halos
        hop = product(before[3].T, before[0]).astype(jnp.bfloat16)
        added[0] = through(hop, before[1], before[2])
        hop = product(coupling[last], after[0]).astype(jnp.bfloat16)
        added[last] = through(hop, after[1], after[2])
    row_ids = lax.broadcasted_iota(jnp.int32, (orbitals, orbitals), 0)
    column_ids = lax.broadcasted_iota(jnp.int32, (orbitals, orbitals), 1)
    on_diagonal = row_ids == column_ids
    sequence = [*range(1, last), 0, last]
    halves, kinds = {}, {}
    for block in sequence:
        middle = source[block]
        if block in added:
            middle = middle + added[block]
        middle = middle.astype(jnp.bfloat16)
        middle = jnp.concatenate([middle[:orbitals], middle[orbitals:]], 1)
        halves[block] = product(green[block], middle).astype(jnp.bfloat16)
    for block in sequence:
        half = halves[block]
        stacked = jnp.concatenate([half[:, :orbitals], half[:, orbitals:]], 0)
        result = product_t(stacked, green[block]) * open_mask[block : block + 1]
        kinds[block] = [result[:orbitals], result[orbitals:]]
        total = sum(kind.astype(jnp.bfloat16).astype(jnp.float32) for kind in kinds[block])
        diagonal[block : block + 1] = jnp.sum(
            jnp.where(on_diagonal, total, 0.0), axis=0, keepdims=True
        )
        if not split:
            for kind in range(2):
                outgoing[kind, block] = kinds[block][kind].astype(jnp.bfloat16)
    if split:
        devices, _, rows, _ = outgoing.shape
        rows //= block_count
        for block in range(0, block_count, 2):
            for kind in range(2):
                for spot, device in enumerate(order):
                    piece = slice(device * rows, (device + 1) * rows)
                    pair = [kinds[block + step][kind][piece] for step in range(2)]
                    outgoing[spot, kind, block * rows : (block + 2) * rows] = jnp.concatenate(
                        pair, 0
                    ).astype(jnp.bfloat16)


def spread(strength, rows):
    return jnp.concatenate([strength] * (rows // strength.shape[0]), 0)


def current_kernel(order, back_order, shift, rows, strength, parts, wide, total):
    energies, _, row_count, orbitals = rows.shape
    block_count = total.shape[1]
    pad = energies // 2
    edge = jnp.zeros((pad, 2, row_count, orbitals), jnp.float32)
    wide[0:pad] = edge
    wide[pad + energies :] = edge
    for spot, energy in enumerate(order):
        wide[pad + energy] = rows[spot].astype(jnp.float32)
    scale = spread(strength[...] * (1.0 / orbitals), row_count)
    first, second = shift[0], shift[1]

    def step(energy, carry):
        here = energy + pad
        above, below = (
            [wide[here + first, kind] + wide[here + second, kind] for kind in range(2)],
            [wide[here - first, kind] + wide[here - second, kind] for kind in range(2)],
        )
        gain = (1.0 + phonon_occupation) * above[0] + phonon_occupation * below[0]
        loss = (1.0 + phonon_occupation) * below[1] + phonon_occupation * above[1]
        flow = (gain * wide[here, 1] - loss * wide[here, 0]) * scale
        total[energy] = jnp.sum(flow.reshape(block_count, -1, orbitals), axis=1)
        return carry

    lax.fori_loop(0, energies, step, 0, unroll=4)
    summed = total[...].reshape(energies * block_count, orbitals)
    coarse = summed.astype(jnp.bfloat16)
    fine = (summed - coarse.astype(jnp.float32)).astype(jnp.bfloat16)
    ones = jnp.ones((8, 2 * orbitals), jnp.bfloat16)
    flat = product_t(ones, jnp.concatenate([coarse, fine], 1))
    for spot, energy in enumerate(back_order):
        parts[spot] = flat[0:1, energy * block_count : (energy + 1) * block_count]


def sigma_kernel(order, shift, arrived, strength, less_out, great_out, rows):
    energies = rows.shape[0]
    for spot, energy in enumerate(order):
        rows[energy] = arrived[spot]
    factor = spread(strength[...], rows.shape[2])

    def step(energy, carry):
        less_sum, great_sum = 0.0, 0.0
        for branch in range(2):
            above, below = energy + shift[branch], energy - shift[branch]
            has_above = (above < energies).astype(jnp.float32)
            has_below = (below >= 0).astype(jnp.float32)
            above = jnp.minimum(above, energies - 1)
            below = jnp.maximum(below, 0)
            more, fewer = 1.0 + phonon_occupation, phonon_occupation
            less_sum = (
                less_sum
                + (more * has_above) * rows[above, 0].astype(jnp.float32)
                + (fewer * has_below) * rows[below, 0].astype(jnp.float32)
            )
            great_sum = (
                great_sum
                + (more * has_below) * rows[below, 1].astype(jnp.float32)
                + (fewer * has_above) * rows[above, 1].astype(jnp.float32)
            )
        less_out[energy] = (factor * less_sum).astype(less_out.dtype)
        great_out[energy] = (factor * great_sum).astype(great_out.dtype)
        return carry

    lax.fori_loop(0, energies, step, 0)


def local(
    green_ret, prior_less, prior_great, coupling, phonon_coupling, phonon_shift, active_blocks
):
    _, block_count, orbitals, _ = green_ret.shape
    devices, places = lax.axis_size("energy"), lax.axis_size("space")
    row_count = orbitals // devices
    last = block_count - 1
    order, back_order = orders(devices)
    swap = places == 2
    if swap:
        edges = [lambda: last * (1 - lax.axis_index("space"))]
    elif places > 1:
        edges = [lambda: last, lambda: 0]
    else:
        edges = []
    arrays, shift, open_mask, packed = load(
        edges, (green_ret, prior_less, prior_great, coupling), active_blocks, phonon_shift
    )
    green, less, great, coupling = arrays
    if swap:
        halos = (lax.ppermute(packed[0], "space", [(0, 1), (1, 0)]),)
    else:
        halos = tuple(
            shifted(edge, "space", step) for edge, step in zip(packed, (1, -1), strict=False)
        )
    source = pl.pallas_call(
        hop_kernel,
        out_shape=held((block_count, 2 * orbitals, orbitals), jnp.float32),
        in_specs=[VMEM] * 4,
        out_specs=VMEM,
        compiler_params=params(),
        cost_estimate=pl.CostEstimate(
            flops=20 * block_count * orbitals**3,
            bytes_accessed=8 * block_count * orbitals**2,
            transcendentals=0,
        ),
    )(green, less, great, coupling)
    split = row_count % 8 == 0 and block_count % 2 == 0
    if split:
        out_shape = (devices, 2, block_count * row_count, orbitals)
    else:
        out_shape = (2, block_count, orbitals, orbitals)
    outgoing, diagonal = pl.pallas_call(
        functools.partial(green_kernel, swap, split, order),
        out_shape=(
            held(out_shape, jnp.bfloat16),
            jax.ShapeDtypeStruct((block_count, orbitals), jnp.float32),
        ),
        in_specs=[VMEM] * (4 + len(halos)),
        out_specs=(VMEM, VMEM),
        compiler_params=params(),
    )(green, coupling, source, open_mask, *halos)
    if not split:
        outgoing = outgoing.reshape(2, block_count, devices, row_count, orbitals)
        outgoing = jnp.stack([outgoing[:, :, device] for device in order])
        outgoing = outgoing.reshape(devices, 2, block_count * row_count, orbitals)
    ldos = jnp.sum(diagonal, axis=1)[None, :] / orbitals
    rows = exchange(outgoing, order)
    parts = pl.pallas_call(
        functools.partial(current_kernel, order, back_order),
        out_shape=held((devices, 1, block_count), jnp.float32),
        in_specs=[SMEM, VMEM, VMEM],
        out_specs=VMEM,
        scratch_shapes=[
            pltpu.VMEM((2 * devices, *rows.shape[1:]), jnp.float32),
            pltpu.VMEM((devices, block_count, orbitals), jnp.float32),
        ],
        compiler_params=params(),
    )(in_smem(shift), rows, phonon_coupling)
    parts = exchange(parts, back_order)
    out = jax.ShapeDtypeStruct((devices, block_count * row_count, orbitals), jnp.bfloat16)
    sigmas = pl.pallas_call(
        functools.partial(sigma_kernel, order),
        out_shape=(out, out),
        in_specs=[SMEM, VMEM, VMEM],
        out_specs=(VMEM, VMEM),
        scratch_shapes=[pltpu.VMEM(rows.shape, rows.dtype)],
        compiler_params=params(),
        cost_estimate=pl.CostEstimate(
            flops=20 * rows.size, bytes_accessed=4 * rows.size, transcendentals=0
        ),
    )(in_smem(shift), rows, phonon_coupling)
    sigma_l, sigma_g = [
        sigma.reshape(devices, block_count, row_count, orbitals) for sigma in sigmas
    ]
    current = jnp.sum(parts, axis=0)
    return (sigma_l, sigma_g, current, ldos)


def solution(mesh):
    return jax.shard_map(
        local,
        mesh=mesh,
        in_specs=(
            P("energy", "space", None, None),
            P("energy", "space", None, None),
            P("energy", "space", None, None),
            P("space", None, None),
            P("energy", None),
            P(),
            P(),
        ),
        out_specs=(
            P(None, "space", "energy", None),
            P(None, "space", "energy", None),
            P("energy", "space"),
            P("energy", "space"),
        ),
        check_vma=False,
    )
```

```python
import functools

import jax
import jax.numpy as jnp
from jax import lax
from jax.experimental import pallas as pl
from jax.experimental.pallas import tpu as pltpu
from jax.sharding import PartitionSpec as P

phonon_occupation = 0.5

VMEM = pl.BlockSpec(memory_space=pltpu.VMEM)
SMEM = pl.BlockSpec(memory_space=pltpu.SMEM)
ANY = pl.BlockSpec(memory_space=pl.ANY)


def shifted(value, axis, steps):
    count = lax.axis_size(axis)
    initial, last = (max(0, -steps), min(count, count - steps))
    return lax.ppermute(value, axis, [(source, source + steps) for source in range(initial, last)])


def orders(count):
    def starting(root):
        return [root] + [index for index in range(count) if index != root]

    return starting(9 * count // 16), starting(count - 1)


def exchange(chunks, order):
    return lax.all_to_all(
        chunks, "energy", split_axis=0, concat_axis=0, tiled=True, axis_index_groups=[order]
    )


def params():
    return pltpu.CompilerParams(vmem_limit_bytes=24 * 1024 * 1024)


def product(left, right):
    return jnp.dot(left, right, preferred_element_type=jnp.float32)


def product_t(left, right):
    return lax.dot_general(
        left, right, (((1,), (1,)), ((), ())), preferred_element_type=jnp.float32
    )


def held(shape, dtype):
    return pltpu.VMEM(shape, dtype)


def in_hbm(*arrays):
    return [pltpu.with_memory_space_constraint(array, pltpu.HBM) for array in arrays]


def in_smem(array):
    return pltpu.with_memory_space_constraint(array, pltpu.SMEM)


def load_kernel(edges, *refs):
    inputs, active, shift = refs[:4], refs[4], refs[5]
    outputs, steps, open_mask = refs[6:10], refs[10], refs[11]
    packed, counts, sems = refs[12 : 12 + len(edges)], refs[-2], refs[-1]
    blocks = [ref if ref.ndim == 3 else ref.at[0] for ref in inputs]
    pairs = [(active, counts), (shift, steps)]
    for block_of, target in zip(edges, packed):
        block = block_of()
        pairs += [(ref.at[block], target.at[slot]) for slot, ref in enumerate(blocks)]
    pairs += list(zip(blocks, outputs))
    copies = [
        pltpu.make_async_copy(origin, target, sems.at[index])
        for index, (origin, target) in enumerate(pairs)
    ]
    for copy in copies:
        copy.start()
    for copy in copies:
        copy.wait()
    block_count = open_mask.shape[0]
    open_count = counts[lax.axis_index("energy")] - lax.axis_index("space") * block_count
    block_ids = lax.broadcasted_iota(jnp.int32, open_mask.shape, 0)
    open_mask[...] = (block_ids < open_count).astype(jnp.float32)


def load(edges, arrays, active, shift):
    _, block_count, orbitals, _ = arrays[0].shape
    blocks = held((block_count, orbitals, orbitals), jnp.bfloat16)
    edge = held((len(arrays), orbitals, orbitals), jnp.bfloat16)
    copies = len(arrays) * (1 + len(edges)) + 2
    results = pl.pallas_call(
        functools.partial(load_kernel, edges),
        out_shape=(
            *[blocks] * len(arrays),
            pltpu.SMEM(shift.shape, shift.dtype),
            held((block_count, orbitals), jnp.float32),
            *[edge] * len(edges),
        ),
        in_specs=[ANY] * (len(arrays) + 2),
        out_specs=(*[VMEM] * len(arrays), SMEM, VMEM, *[VMEM] * len(edges)),
        scratch_shapes=[
            pltpu.SMEM(active.shape, active.dtype),
            pltpu.SemaphoreType.DMA((copies,)),
        ],
        compiler_params=params(),
    )(*in_hbm(*arrays, active, shift))
    kept = len(arrays)
    return results[:kept], results[kept], results[kept + 1], results[kept + 2 :]


def through(operator, less, great):
    rows = operator.shape[0]
    half = product(operator, jnp.concatenate([less, great], 1)).astype(jnp.bfloat16)
    stacked = jnp.concatenate([half[:, :rows], half[:, rows:]], 0)
    return product_t(stacked, operator)


def finish(blocks, middles, green, open_mask, outgoing, order):
    orbitals = green.shape[1]
    halves, kinds = {}, {}
    for block in blocks:
        middle = middles[block].astype(jnp.bfloat16)
        middle = jnp.concatenate([middle[:orbitals], middle[orbitals:]], 1)
        halves[block] = product(green[block], middle).astype(jnp.bfloat16)
    for block in blocks:
        half = halves[block]
        stacked = jnp.concatenate([half[:, :orbitals], half[:, orbitals:]], 0)
        result = product_t(stacked, green[block]) * open_mask[block : block + 1]
        kinds[block] = [result[:orbitals], result[orbitals:]]
    for block in blocks:
        for kind in range(2):
            if order is None:
                outgoing[kind, block] = kinds[block][kind].astype(jnp.bfloat16)
            elif block % 2 == 0:
                rows = orbitals // len(order)
                for spot, device in enumerate(order):
                    piece = slice(device * rows, (device + 1) * rows)
                    pair = [kinds[block + step][kind][piece] for step in range(2)]
                    outgoing[spot, kind, block * rows : (block + 2) * rows] = jnp.concatenate(
                        pair, 0
                    ).astype(jnp.bfloat16)


def hop_kernel(outer, order, green, less, great, coupling, open_mask, source, outgoing):
    block_count, orbitals = green.shape[0], green.shape[1]
    blocks = range(block_count)
    hops, both, middles = [], [], []
    for block in blocks:
        factors = []
        if block + 1 < block_count:
            factors.append(coupling[block].T)
        if block > 0:
            factors.append(coupling[block - 1])
        hops.append(product(jnp.concatenate(factors, 0), green[block]).astype(jnp.bfloat16))
    for block in blocks:
        prior = jnp.concatenate([less[block], great[block]], 1)
        both.append(product(hops[block], prior).astype(jnp.bfloat16))
        middles.append(jnp.concatenate([less[block], great[block]], 0).astype(jnp.float32))
    for block in blocks:
        first = 0
        for target in (block + 1, block - 1):
            if 0 <= target < block_count:
                piece = slice(first, first + orbitals)
                half = both[block][piece]
                stacked = jnp.concatenate([half[:, :orbitals], half[:, orbitals:]], 0)
                middles[target] = middles[target] + product_t(stacked, hops[block][piece])
                first += orbitals
    for slot, block in enumerate(outer):
        source[slot] = middles[block]
    inner = [block for block in blocks if block not in outer]
    finish(inner, middles, green, open_mask, outgoing, order)


def green_kernel(swap, outer, order, green, coupling, open_mask, source, _, *rest):
    halos, outgoing = rest[:-1], rest[-1]
    last = green.shape[0] - 1
    place = lax.axis_index("space")
    middles = {block: source[slot] for slot, block in enumerate(outer)}
    if swap:
        (halo,) = halos
        hop = jnp.where(place == 0, coupling[last], halo[3].T)
        edge = through(product(hop, halo[0]).astype(jnp.bfloat16), halo[1], halo[2])
        middles[0] = middles[0] + jnp.where(place > 0, edge, 0.0)
        middles[last] = middles[last] + jnp.where(place == 0, edge, 0.0)
    elif halos:
        before, after = halos
        hop = product(before[3].T, before[0]).astype(jnp.bfloat16)
        middles[0] = middles[0] + through(hop, before[1], before[2])
        hop = product(coupling[last], after[0]).astype(jnp.bfloat16)
        middles[last] = middles[last] + through(hop, after[1], after[2])
    finish(outer, middles, green, open_mask, outgoing, order)


def lane_sums(values):
    coarse = values.astype(jnp.bfloat16)
    fine = (values - coarse.astype(jnp.float32)).astype(jnp.bfloat16)
    ones = jnp.ones((8, 2 * values.shape[1]), jnp.bfloat16)
    return product_t(ones, jnp.concatenate([coarse, fine], 1))[0:1]


def density_kernel(order, rows, density):
    _, _, row_count, orbitals = rows.shape
    block_count = density.shape[1]
    local_rows = row_count // block_count
    row_ids = lax.broadcasted_iota(jnp.int32, (row_count, orbitals), 0) % local_rows
    column_ids = lax.broadcasted_iota(jnp.int32, (row_count, orbitals), 1)
    total = jnp.zeros((row_count, orbitals), jnp.float32)
    for spot, device in enumerate(order):
        both = rows[spot, 0].astype(jnp.float32) + rows[spot, 1].astype(jnp.float32)
        total = jnp.where(column_ids == row_ids + device * local_rows, both, total)
    total = jnp.sum(total.reshape(block_count, local_rows, orbitals), axis=1)
    density[...] = lane_sums(total) / orbitals


def spread(strength, rows):
    return jnp.concatenate([strength] * (rows // strength.shape[0]), 0)


def current_kernel(order, back_order, shift, rows, strength, parts, wide, total):
    energies, _, row_count, orbitals = rows.shape
    block_count = total.shape[1]
    pad = energies // 2
    edge = jnp.zeros((pad, 2, row_count, orbitals), jnp.float32)
    wide[0:pad] = edge
    wide[pad + energies :] = edge
    for spot, energy in enumerate(order):
        wide[pad + energy] = rows[spot].astype(jnp.float32)
    scale = spread(strength[...] * (1.0 / orbitals), row_count)
    first, second = shift[0], shift[1]

    def step(energy, carry):
        here = energy + pad
        above, below = (
            [wide[here + first, kind] + wide[here + second, kind] for kind in range(2)],
            [wide[here - first, kind] + wide[here - second, kind] for kind in range(2)],
        )
        gain = (1.0 + phonon_occupation) * above[0] + phonon_occupation * below[0]
        loss = (1.0 + phonon_occupation) * below[1] + phonon_occupation * above[1]
        flow = (gain * wide[here, 1] - loss * wide[here, 0]) * scale
        total[energy] = jnp.sum(flow.reshape(block_count, -1, orbitals), axis=1)
        return carry

    lax.fori_loop(0, energies, step, 0, unroll=4)
    flat = lane_sums(total[...].reshape(energies * block_count, orbitals))
    for spot, energy in enumerate(back_order):
        parts[spot] = flat[:, energy * block_count : (energy + 1) * block_count]


def sigma_kernel(pieces, shift, wide, strength, less_out, great_out, less, great, sems):
    energies, row_count, _ = less.shape
    pad = energies // 2
    factor = spread(strength[...], row_count)
    first, second = shift[0], shift[1]

    def step(energy, carry):
        here = energy + pad
        above, below = (
            [wide[here + first, kind] + wide[here + second, kind] for kind in range(2)],
            [wide[here - first, kind] + wide[here - second, kind] for kind in range(2)],
        )
        gain = (1.0 + phonon_occupation) * above[0] + phonon_occupation * below[0]
        loss = (1.0 + phonon_occupation) * below[1] + phonon_occupation * above[1]
        less[energy] = (factor * gain).astype(less.dtype)
        great[energy] = (factor * loss).astype(great.dtype)
        return carry

    copies = []
    length = energies // pieces
    for piece in range(pieces):
        lax.fori_loop(piece * length, (piece + 1) * length, step, 0, unroll=2)
        part = pl.ds(piece * length, length)
        for slot, (origin, target) in enumerate(((less, less_out), (great, great_out))):
            copy = pltpu.make_async_copy(origin.at[part], target.at[part], sems.at[slot, piece])
            copy.start()
            copies.append(copy)
    for copy in copies:
        copy.wait()


def local(
    green_ret, prior_less, prior_great, coupling, phonon_coupling, phonon_shift, active_blocks
):
    _, block_count, orbitals, _ = green_ret.shape
    devices, places = lax.axis_size("energy"), lax.axis_size("space")
    row_count = orbitals // devices
    last = block_count - 1
    order, back_order = orders(devices)
    swap = places == 2
    if swap:
        edges = [lambda: last * (1 - lax.axis_index("space"))]
    elif places > 1:
        edges = [lambda: last, lambda: 0]
    else:
        edges = []
    arrays, shift, open_mask, packed = load(
        edges, (green_ret, prior_less, prior_great, coupling), active_blocks, phonon_shift
    )
    green, less, great, coupling = arrays
    if swap:
        halos = (lax.ppermute(packed[0], "space", [(0, 1), (1, 0)]),)
    else:
        halos = tuple(
            shifted(edge, "space", step) for edge, step in zip(packed, (1, -1), strict=False)
        )
    split = row_count % 8 == 0 and block_count % 2 == 0
    if split:
        out_shape = (devices, 2, block_count * row_count, orbitals)
    else:
        out_shape = (2, block_count, orbitals, orbitals)
    outer = sorted({0, 1, last - 1, last})
    store_order = order if split else None
    source, outgoing = pl.pallas_call(
        functools.partial(hop_kernel, outer, store_order),
        out_shape=(
            held((len(outer), 2 * orbitals, orbitals), jnp.float32),
            held(out_shape, jnp.bfloat16),
        ),
        in_specs=[VMEM] * 5,
        out_specs=(VMEM, VMEM),
        compiler_params=params(),
        cost_estimate=pl.CostEstimate(
            flops=20 * block_count * orbitals**3,
            bytes_accessed=8 * block_count * orbitals**2,
            transcendentals=0,
        ),
    )(green, less, great, coupling, open_mask)
    outgoing = pl.pallas_call(
        functools.partial(green_kernel, swap, outer, store_order),
        out_shape=held(out_shape, jnp.bfloat16),
        in_specs=[VMEM] * (5 + len(halos)),
        out_specs=VMEM,
        input_output_aliases={4: 0},
        compiler_params=params(),
    )(green, coupling, open_mask, source, outgoing, *halos)
    if not split:
        outgoing = outgoing.reshape(2, block_count, devices, row_count, orbitals)
        outgoing = jnp.stack([outgoing[:, :, device] for device in order])
        outgoing = outgoing.reshape(devices, 2, block_count * row_count, orbitals)
    rows = exchange(outgoing, order)
    ldos = pl.pallas_call(
        functools.partial(density_kernel, order),
        out_shape=jax.ShapeDtypeStruct((1, block_count), jnp.float32),
        in_specs=[VMEM],
        out_specs=VMEM,
        compiler_params=params(),
        cost_estimate=pl.CostEstimate(
            flops=4 * rows.size, bytes_accessed=2 * rows.size, transcendentals=0
        ),
    )(outgoing)
    parts, wide = pl.pallas_call(
        functools.partial(current_kernel, order, back_order),
        out_shape=(
            held((devices, 1, block_count), jnp.float32),
            held((2 * devices, *rows.shape[1:]), jnp.float32),
        ),
        in_specs=[SMEM, VMEM, VMEM],
        out_specs=(VMEM, VMEM),
        scratch_shapes=[pltpu.VMEM((devices, block_count, orbitals), jnp.float32)],
        compiler_params=params(),
    )(in_smem(shift), rows, phonon_coupling)
    parts = exchange(parts, back_order)
    out_shape = (devices, block_count * row_count, orbitals)
    pieces = 4 if devices % 4 == 0 else 1
    sigmas = pl.pallas_call(
        functools.partial(sigma_kernel, pieces),
        out_shape=[pltpu.HBM(out_shape, jnp.bfloat16)] * 2,
        in_specs=[SMEM, VMEM, VMEM],
        out_specs=[ANY] * 2,
        scratch_shapes=[
            *[pltpu.VMEM(out_shape, jnp.bfloat16)] * 2,
            pltpu.SemaphoreType.DMA((2, pieces)),
        ],
        compiler_params=params(),
        cost_estimate=pl.CostEstimate(
            flops=20 * rows.size, bytes_accessed=4 * rows.size, transcendentals=0
        ),
    )(in_smem(shift), wide, phonon_coupling)
    sigma_l, sigma_g = [
        sigma.reshape(devices, block_count, row_count, orbitals) for sigma in sigmas
    ]
    current = jnp.sum(parts, axis=0)
    return (sigma_l, sigma_g, current, ldos)


def solution(mesh):
    return jax.shard_map(
        local,
        mesh=mesh,
        in_specs=(
            P("energy", "space", None, None),
            P("energy", "space", None, None),
            P("energy", "space", None, None),
            P("space", None, None),
            P("energy", None),
            P(),
            P(),
        ),
        out_specs=(
            P(None, "space", "energy", None),
            P(None, "space", "energy", None),
            P("energy", "space"),
            P("energy", "space"),
        ),
        check_vma=False,
    )
```

```python
import functools

import jax
import jax.numpy as jnp
from jax import lax
from jax.experimental import pallas as pl
from jax.experimental.pallas import tpu as pltpu
from jax.sharding import PartitionSpec as P

phonon_occupation = 0.5

VMEM = pl.BlockSpec(memory_space=pltpu.VMEM)
SMEM = pl.BlockSpec(memory_space=pltpu.SMEM)
ANY = pl.BlockSpec(memory_space=pl.ANY)


def shifted(value, axis, steps):
    count = lax.axis_size(axis)
    initial, last = (max(0, -steps), min(count, count - steps))
    return lax.ppermute(value, axis, [(source, source + steps) for source in range(initial, last)])


def orders(count):
    def starting(root):
        return [root] + [index for index in range(count) if index != root]

    return starting(11 * count // 16), starting(count - 1)


def exchange(chunks, order):
    return lax.all_to_all(
        chunks, "energy", split_axis=0, concat_axis=0, tiled=True, axis_index_groups=[order]
    )


def params():
    return pltpu.CompilerParams(vmem_limit_bytes=24 * 1024 * 1024)


def product(left, right):
    return jnp.dot(left, right, preferred_element_type=jnp.float32)


def product_t(left, right):
    return lax.dot_general(
        left, right, (((1,), (1,)), ((), ())), preferred_element_type=jnp.float32
    )


def held(shape, dtype):
    return pltpu.VMEM(shape, dtype)


def in_hbm(*arrays):
    return [pltpu.with_memory_space_constraint(array, pltpu.HBM) for array in arrays]


def in_smem(array):
    return pltpu.with_memory_space_constraint(array, pltpu.SMEM)


def load_kernel(edges, *refs):
    inputs, active, shift = refs[:4], refs[4], refs[5]
    outputs, steps, open_mask = refs[6:10], refs[10], refs[11]
    packed, counts, sems = refs[12 : 12 + len(edges)], refs[-2], refs[-1]
    blocks = [ref if ref.ndim == 3 else ref.at[0] for ref in inputs]
    pairs = [(active, counts), (shift, steps)]
    for block_of, target in zip(edges, packed):
        block = block_of()
        pairs += [(ref.at[block], target.at[slot]) for slot, ref in enumerate(blocks)]
    pairs += list(zip(blocks, outputs))
    copies = [
        pltpu.make_async_copy(origin, target, sems.at[index])
        for index, (origin, target) in enumerate(pairs)
    ]
    for copy in copies:
        copy.start()
    for copy in copies:
        copy.wait()
    block_count = open_mask.shape[0]
    open_count = counts[lax.axis_index("energy")] - lax.axis_index("space") * block_count
    block_ids = lax.broadcasted_iota(jnp.int32, open_mask.shape, 0)
    open_mask[...] = (block_ids < open_count).astype(jnp.float32)


def load(edges, arrays, active, shift):
    _, block_count, orbitals, _ = arrays[0].shape
    blocks = held((block_count, orbitals, orbitals), jnp.bfloat16)
    edge = held((len(arrays), orbitals, orbitals), jnp.bfloat16)
    copies = len(arrays) * (1 + len(edges)) + 2
    results = pl.pallas_call(
        functools.partial(load_kernel, edges),
        out_shape=(
            *[blocks] * len(arrays),
            pltpu.SMEM(shift.shape, shift.dtype),
            held((block_count, orbitals), jnp.float32),
            *[edge] * len(edges),
        ),
        in_specs=[ANY] * (len(arrays) + 2),
        out_specs=(*[VMEM] * len(arrays), SMEM, VMEM, *[VMEM] * len(edges)),
        scratch_shapes=[
            pltpu.SMEM(active.shape, active.dtype),
            pltpu.SemaphoreType.DMA((copies,)),
        ],
        compiler_params=params(),
    )(*in_hbm(*arrays, active, shift))
    kept = len(arrays)
    return results[:kept], results[kept], results[kept + 1], results[kept + 2 :]


def through(operator, less, great):
    rows = operator.shape[0]
    half = product(operator, jnp.concatenate([less, great], 1)).astype(jnp.bfloat16)
    stacked = jnp.concatenate([half[:, :rows], half[:, rows:]], 0)
    return product_t(stacked, operator)


def finish(blocks, middles, green, open_mask, outgoing, diagonal, order):
    orbitals = green.shape[1]
    row_ids = lax.broadcasted_iota(jnp.int32, (orbitals, orbitals), 0)
    on_diagonal = row_ids == lax.broadcasted_iota(jnp.int32, (orbitals, orbitals), 1)
    halves, kinds = {}, {}
    for block in blocks:
        middle = middles[block].astype(jnp.bfloat16)
        middle = jnp.concatenate([middle[:orbitals], middle[orbitals:]], 1)
        halves[block] = product(green[block], middle).astype(jnp.bfloat16)
    for block in blocks:
        half = halves[block]
        stacked = jnp.concatenate([half[:, :orbitals], half[:, orbitals:]], 0)
        result = product_t(stacked, green[block]) * open_mask[block : block + 1]
        kinds[block] = [result[:orbitals], result[orbitals:]]
        diagonal[block : block + 1] = jnp.sum(
            jnp.where(on_diagonal, kinds[block][0] + kinds[block][1], 0.0), axis=0, keepdims=True
        )
    for block in blocks:
        for kind in range(2):
            if order is None:
                outgoing[kind, block] = kinds[block][kind].astype(jnp.bfloat16)
            elif block % 2 == 0:
                rows = orbitals // len(order)
                for spot, device in enumerate(order):
                    piece = slice(device * rows, (device + 1) * rows)
                    pair = [kinds[block + step][kind][piece] for step in range(2)]
                    outgoing[spot, kind, block * rows : (block + 2) * rows] = jnp.concatenate(
                        pair, 0
                    ).astype(jnp.bfloat16)


def hop_kernel(outer, order, green, less, great, coupling, open_mask, source, outgoing, diagonal):
    block_count, orbitals = green.shape[0], green.shape[1]
    blocks = range(block_count)
    hops, both, middles = [], [], []
    for block in blocks:
        factors = []
        if block + 1 < block_count:
            factors.append(coupling[block].T)
        if block > 0:
            factors.append(coupling[block - 1])
        hops.append(product(jnp.concatenate(factors, 0), green[block]).astype(jnp.bfloat16))
    for block in blocks:
        prior = jnp.concatenate([less[block], great[block]], 1)
        both.append(product(hops[block], prior).astype(jnp.bfloat16))
        middles.append(jnp.concatenate([less[block], great[block]], 0).astype(jnp.float32))
    for block in blocks:
        first = 0
        for target in (block + 1, block - 1):
            if 0 <= target < block_count:
                piece = slice(first, first + orbitals)
                half = both[block][piece]
                stacked = jnp.concatenate([half[:, :orbitals], half[:, orbitals:]], 0)
                middles[target] = middles[target] + product_t(stacked, hops[block][piece])
                first += orbitals
    for slot, block in enumerate(outer):
        source[slot] = middles[block]
    inner = [block for block in blocks if block not in outer]
    finish(inner, middles, green, open_mask, outgoing, diagonal, order)


def green_kernel(swap, outer, order, green, coupling, open_mask, source, *rest):
    (_, inner_diagonal), halos, (outgoing, diagonal) = rest[:2], rest[2:-2], rest[-2:]
    last = green.shape[0] - 1
    place = lax.axis_index("space")
    middles = {block: source[slot] for slot, block in enumerate(outer)}
    if swap:
        (halo,) = halos
        hop = jnp.where(place == 0, coupling[last], halo[3].T)
        edge = through(product(hop, halo[0]).astype(jnp.bfloat16), halo[1], halo[2])
        middles[0] = middles[0] + jnp.where(place > 0, edge, 0.0)
        middles[last] = middles[last] + jnp.where(place == 0, edge, 0.0)
    elif halos:
        before, after = halos
        hop = product(before[3].T, before[0]).astype(jnp.bfloat16)
        middles[0] = middles[0] + through(hop, before[1], before[2])
        hop = product(coupling[last], after[0]).astype(jnp.bfloat16)
        middles[last] = middles[last] + through(hop, after[1], after[2])
    diagonal[...] = inner_diagonal[...]
    finish(outer, middles, green, open_mask, outgoing, diagonal, order)


def lane_sums(values):
    coarse = values.astype(jnp.bfloat16)
    fine = (values - coarse.astype(jnp.float32)).astype(jnp.bfloat16)
    ones = jnp.ones((8, 2 * values.shape[1]), jnp.bfloat16)
    return product_t(ones, jnp.concatenate([coarse, fine], 1))[0:1]


def totals_kernel(parts, diagonal, less, great, current, density, less_out, great_out, sems):
    copies = [
        pltpu.make_async_copy(less, less_out, sems.at[0]),
        pltpu.make_async_copy(great, great_out, sems.at[1]),
    ]
    for copy in copies:
        copy.start()
    total = parts[0]
    for spot in range(1, parts.shape[0]):
        total = total + parts[spot]
    current[...] = total
    density[...] = lane_sums(diagonal[...]) / diagonal.shape[1]
    for copy in copies:
        copy.wait()


def spread(strength, rows):
    return jnp.concatenate([strength] * (rows // strength.shape[0]), 0)


def current_kernel(order, back_order, shift, rows, strength, parts, less, great, wide, total):
    energies, _, row_count, orbitals = rows.shape
    block_count = total.shape[1]
    pad = energies // 2
    edge = jnp.zeros((pad, 2, row_count, orbitals), jnp.float32)
    wide[0:pad] = edge
    wide[pad + energies :] = edge
    for spot, energy in enumerate(order):
        wide[pad + energy] = rows[spot].astype(jnp.float32)
    factor = spread(strength[...], row_count)
    scale = spread(strength[...] * (1.0 / orbitals), row_count)
    first, second = shift[0], shift[1]

    def step(energy, carry):
        here = energy + pad
        above, below = (
            [wide[here + first, kind] + wide[here + second, kind] for kind in range(2)],
            [wide[here - first, kind] + wide[here - second, kind] for kind in range(2)],
        )
        gain = (1.0 + phonon_occupation) * above[0] + phonon_occupation * below[0]
        loss = (1.0 + phonon_occupation) * below[1] + phonon_occupation * above[1]
        less[energy] = (factor * gain).astype(less.dtype)
        great[energy] = (factor * loss).astype(great.dtype)
        flow = (gain * wide[here, 1] - loss * wide[here, 0]) * scale
        total[energy] = jnp.sum(flow.reshape(block_count, -1, orbitals), axis=1)
        return carry

    lax.fori_loop(0, energies, step, 0, unroll=4)
    flat = lane_sums(total[...].reshape(energies * block_count, orbitals))
    for spot, energy in enumerate(back_order):
        parts[spot] = flat[:, energy * block_count : (energy + 1) * block_count]


def local(
    green_ret, prior_less, prior_great, coupling, phonon_coupling, phonon_shift, active_blocks
):
    _, block_count, orbitals, _ = green_ret.shape
    devices, places = lax.axis_size("energy"), lax.axis_size("space")
    row_count = orbitals // devices
    last = block_count - 1
    order, back_order = orders(devices)
    swap = places == 2
    if swap:
        edges = [lambda: last * (1 - lax.axis_index("space"))]
    elif places > 1:
        edges = [lambda: last, lambda: 0]
    else:
        edges = []
    arrays, shift, open_mask, packed = load(
        edges, (green_ret, prior_less, prior_great, coupling), active_blocks, phonon_shift
    )
    green, less, great, coupling = arrays
    if swap:
        halos = (lax.ppermute(packed[0], "space", [(0, 1), (1, 0)]),)
    else:
        halos = tuple(
            shifted(edge, "space", step) for edge, step in zip(packed, (1, -1), strict=False)
        )
    split = row_count % 8 == 0 and block_count % 2 == 0
    if split:
        out_shape = (devices, 2, block_count * row_count, orbitals)
    else:
        out_shape = (2, block_count, orbitals, orbitals)
    outer = sorted({0, 1, last - 1, last})
    store_order = order if split else None
    diagonals = held((block_count, orbitals), jnp.float32)
    source, outgoing, diagonal = pl.pallas_call(
        functools.partial(hop_kernel, outer, store_order),
        out_shape=(
            held((len(outer), 2 * orbitals, orbitals), jnp.float32),
            held(out_shape, jnp.bfloat16),
            diagonals,
        ),
        in_specs=[VMEM] * 5,
        out_specs=(VMEM, VMEM, VMEM),
        compiler_params=params(),
        cost_estimate=pl.CostEstimate(
            flops=20 * block_count * orbitals**3,
            bytes_accessed=8 * block_count * orbitals**2,
            transcendentals=0,
        ),
    )(green, less, great, coupling, open_mask)
    outgoing, diagonal = pl.pallas_call(
        functools.partial(green_kernel, swap, outer, store_order),
        out_shape=(held(out_shape, jnp.bfloat16), diagonals),
        in_specs=[VMEM] * (6 + len(halos)),
        out_specs=(VMEM, VMEM),
        input_output_aliases={4: 0},
        compiler_params=params(),
    )(green, coupling, open_mask, source, outgoing, diagonal, *halos)
    if not split:
        outgoing = outgoing.reshape(2, block_count, devices, row_count, orbitals)
        outgoing = jnp.stack([outgoing[:, :, device] for device in order])
        outgoing = outgoing.reshape(devices, 2, block_count * row_count, orbitals)
    rows = exchange(outgoing, order)
    sigma_shape = held((devices, block_count * row_count, orbitals), jnp.bfloat16)
    parts, *sigmas = pl.pallas_call(
        functools.partial(current_kernel, order, back_order),
        out_shape=(held((devices, 1, block_count), jnp.float32), sigma_shape, sigma_shape),
        in_specs=[SMEM, VMEM, VMEM],
        out_specs=(VMEM, VMEM, VMEM),
        scratch_shapes=[
            pltpu.VMEM((2 * devices, *rows.shape[1:]), jnp.float32),
            pltpu.VMEM((devices, block_count, orbitals), jnp.float32),
        ],
        compiler_params=params(),
    )(in_smem(shift), rows, phonon_coupling)
    parts = exchange(parts, back_order)
    sums = jax.ShapeDtypeStruct((1, block_count), jnp.float32)
    sigma_out = pltpu.HBM(sigmas[0].shape, sigmas[0].dtype)
    current, ldos, *sigmas = pl.pallas_call(
        totals_kernel,
        out_shape=(sums, sums, sigma_out, sigma_out),
        in_specs=[VMEM] * 4,
        out_specs=(VMEM, VMEM, ANY, ANY),
        scratch_shapes=[pltpu.SemaphoreType.DMA((2,))],
        compiler_params=params(),
    )(parts, diagonal, *sigmas)
    sigma_l, sigma_g = [
        sigma.reshape(devices, block_count, row_count, orbitals) for sigma in sigmas
    ]
    return (sigma_l, sigma_g, current, ldos)


def solution(mesh):
    return jax.shard_map(
        local,
        mesh=mesh,
        in_specs=(
            P("energy", "space", None, None),
            P("energy", "space", None, None),
            P("energy", "space", None, None),
            P("space", None, None),
            P("energy", None),
            P(),
            P(),
        ),
        out_specs=(
            P(None, "space", "energy", None),
            P(None, "space", "energy", None),
            P("energy", "space"),
            P("energy", "space"),
        ),
        check_vma=False,
    )
```

```python
import functools

import jax
import jax.numpy as jnp
from jax import lax
from jax.experimental import pallas as pl
from jax.experimental.pallas import tpu as pltpu
from jax.sharding import PartitionSpec as P

phonon_occupation = 0.5

VMEM = pl.BlockSpec(memory_space=pltpu.VMEM)
SMEM = pl.BlockSpec(memory_space=pltpu.SMEM)
ANY = pl.BlockSpec(memory_space=pl.ANY)


def shifted(value, axis, steps):
    count = lax.axis_size(axis)
    initial, last = (max(0, -steps), min(count, count - steps))
    return lax.ppermute(value, axis, [(source, source + steps) for source in range(initial, last)])


def orders(count):
    def starting(root):
        return [root] + [index for index in range(count) if index != root]

    return starting(11 * count // 16), starting(count - 1)


def exchange(chunks, order):
    return lax.all_to_all(
        chunks, "energy", split_axis=0, concat_axis=0, tiled=True, axis_index_groups=[order]
    )


def params():
    return pltpu.CompilerParams(vmem_limit_bytes=24 * 1024 * 1024)


def product(left, right):
    return jnp.dot(left, right, preferred_element_type=jnp.float32)


def product_t(left, right):
    return lax.dot_general(
        left, right, (((1,), (1,)), ((), ())), preferred_element_type=jnp.float32
    )


def held(shape, dtype):
    return pltpu.VMEM(shape, dtype)


def in_hbm(*arrays):
    return [pltpu.with_memory_space_constraint(array, pltpu.HBM) for array in arrays]


def in_smem(array):
    return pltpu.with_memory_space_constraint(array, pltpu.SMEM)


def load_kernel(edges, *refs):
    inputs, active, shift = refs[:4], refs[4], refs[5]
    outputs, steps, open_mask = refs[6:10], refs[10], refs[11]
    packed, counts, sems = refs[12 : 12 + len(edges)], refs[-2], refs[-1]
    blocks = [ref if ref.ndim == 3 else ref.at[0] for ref in inputs]
    pairs = [(active, counts), (shift, steps)]
    for block_of, target in zip(edges, packed):
        block = block_of()
        pairs += [(ref.at[block], target.at[slot]) for slot, ref in enumerate(blocks)]
    pairs += list(zip(blocks, outputs))
    copies = [
        pltpu.make_async_copy(origin, target, sems.at[index])
        for index, (origin, target) in enumerate(pairs)
    ]
    for copy in copies:
        copy.start()
    for copy in copies:
        copy.wait()
    block_count = open_mask.shape[0]
    open_count = counts[lax.axis_index("energy")] - lax.axis_index("space") * block_count
    block_ids = lax.broadcasted_iota(jnp.int32, open_mask.shape, 0)
    open_mask[...] = (block_ids < open_count).astype(jnp.float32)


def load(edges, arrays, active, shift):
    _, block_count, orbitals, _ = arrays[0].shape
    blocks = held((block_count, orbitals, orbitals), jnp.bfloat16)
    edge = held((len(arrays), orbitals, orbitals), jnp.bfloat16)
    copies = len(arrays) * (1 + len(edges)) + 2
    results = pl.pallas_call(
        functools.partial(load_kernel, edges),
        out_shape=(
            *[blocks] * len(arrays),
            pltpu.SMEM(shift.shape, shift.dtype),
            held((block_count, orbitals), jnp.float32),
            *[edge] * len(edges),
        ),
        in_specs=[ANY] * (len(arrays) + 2),
        out_specs=(*[VMEM] * len(arrays), SMEM, VMEM, *[VMEM] * len(edges)),
        scratch_shapes=[
            pltpu.SMEM(active.shape, active.dtype),
            pltpu.SemaphoreType.DMA((copies,)),
        ],
        compiler_params=params(),
    )(*in_hbm(*arrays, active, shift))
    kept = len(arrays)
    return results[:kept], results[kept], results[kept + 1], results[kept + 2 :]


def through(operator, less, great):
    rows = operator.shape[0]
    half = product(operator, jnp.concatenate([less, great], 1)).astype(jnp.bfloat16)
    stacked = jnp.concatenate([half[:, :rows], half[:, rows:]], 0)
    return product_t(stacked, operator)


def finish(blocks, middles, green, open_mask, outgoing, diagonal, order):
    orbitals = green.shape[1]
    row_ids = lax.broadcasted_iota(jnp.int32, (orbitals, orbitals), 0)
    on_diagonal = row_ids == lax.broadcasted_iota(jnp.int32, (orbitals, orbitals), 1)
    halves, kinds = {}, {}
    for block in blocks:
        middle = middles[block].astype(jnp.bfloat16)
        middle = jnp.concatenate([middle[:orbitals], middle[orbitals:]], 1)
        halves[block] = product(green[block], middle).astype(jnp.bfloat16)
    for block in blocks:
        half = halves[block]
        stacked = jnp.concatenate([half[:, :orbitals], half[:, orbitals:]], 0)
        result = product_t(stacked, green[block]) * open_mask[block : block + 1]
        kinds[block] = [result[:orbitals], result[orbitals:]]
        diagonal[block : block + 1] = jnp.sum(
            jnp.where(on_diagonal, kinds[block][0] + kinds[block][1], 0.0), axis=0, keepdims=True
        )
    for block in blocks:
        for kind in range(2):
            if order is None:
                outgoing[kind, block] = kinds[block][kind].astype(jnp.bfloat16)
            elif block % 2 == 0:
                rows = orbitals // len(order)
                for spot, device in enumerate(order):
                    piece = slice(device * rows, (device + 1) * rows)
                    pair = [kinds[block + step][kind][piece] for step in range(2)]
                    outgoing[spot, kind, block * rows : (block + 2) * rows] = jnp.concatenate(
                        pair, 0
                    ).astype(jnp.bfloat16)


def hop_kernel(outer, order, green, less, great, coupling, open_mask, source, outgoing, diagonal):
    block_count, orbitals = green.shape[0], green.shape[1]
    blocks = range(block_count)
    hops, both, middles = [], [], []
    for block in blocks:
        factors = []
        if block + 1 < block_count:
            factors.append(coupling[block].T)
        if block > 0:
            factors.append(coupling[block - 1])
        hops.append(product(jnp.concatenate(factors, 0), green[block]).astype(jnp.bfloat16))
    for block in blocks:
        prior = jnp.concatenate([less[block], great[block]], 1)
        both.append(product(hops[block], prior).astype(jnp.bfloat16))
        middles.append(jnp.concatenate([less[block], great[block]], 0).astype(jnp.float32))
    for block in blocks:
        sent = []
        if block > 0:
            sent.append((block - 1, slice(0, orbitals)))
        if block + 1 < block_count:
            first = orbitals if block + 2 < block_count else 0
            sent.append((block + 1, slice(first, first + orbitals)))
        stacked = [
            jnp.concatenate([both[origin][piece, kind] for origin, piece in sent], 1)
            for kind in (slice(0, orbitals), slice(orbitals, 2 * orbitals))
        ]
        operators = jnp.concatenate([hops[origin][piece] for origin, piece in sent], 1)
        middles[block] = middles[block] + product_t(jnp.concatenate(stacked, 0), operators)
    for slot, block in enumerate(outer):
        source[slot] = middles[block]
    inner = [block for block in blocks if block not in outer]
    finish(inner, middles, green, open_mask, outgoing, diagonal, order)


def green_kernel(swap, outer, order, green, coupling, open_mask, source, *rest):
    (_, inner_diagonal), halos, (outgoing, diagonal) = rest[:2], rest[2:-2], rest[-2:]
    last = green.shape[0] - 1
    place = lax.axis_index("space")
    middles = {block: source[slot] for slot, block in enumerate(outer)}
    if swap:
        (halo,) = halos
        hop = jnp.where(place == 0, coupling[last], halo[3].T)
        edge = through(product(hop, halo[0]).astype(jnp.bfloat16), halo[1], halo[2])
        middles[0] = middles[0] + jnp.where(place > 0, edge, 0.0)
        middles[last] = middles[last] + jnp.where(place == 0, edge, 0.0)
    elif halos:
        before, after = halos
        hop = product(before[3].T, before[0]).astype(jnp.bfloat16)
        middles[0] = middles[0] + through(hop, before[1], before[2])
        hop = product(coupling[last], after[0]).astype(jnp.bfloat16)
        middles[last] = middles[last] + through(hop, after[1], after[2])
    diagonal[...] = inner_diagonal[...]
    finish(outer, middles, green, open_mask, outgoing, diagonal, order)


def lane_sums(values):
    coarse = values.astype(jnp.bfloat16)
    fine = (values - coarse.astype(jnp.float32)).astype(jnp.bfloat16)
    ones = jnp.ones((8, 2 * values.shape[1]), jnp.bfloat16)
    return product_t(ones, jnp.concatenate([coarse, fine], 1))[0:1]


def copy_out(less, great, less_out, great_out, sems):
    copies = [
        pltpu.make_async_copy(less, less_out, sems.at[0]),
        pltpu.make_async_copy(great, great_out, sems.at[1]),
    ]
    for copy in copies:
        copy.start()
    for copy in copies:
        copy.wait()


def has_time():
    return lax.axis_index("energy") == 0


def totals_kernel(parts, diagonal, less, great, _, __, current, density, *outputs):
    total = parts[0]
    for spot in range(1, parts.shape[0]):
        total = total + parts[spot]
    current[...] = total
    density[...] = lane_sums(diagonal[...]) / diagonal.shape[1]
    pl.when(jnp.logical_not(has_time()))(functools.partial(copy_out, less, great, *outputs))


def spread(strength, rows):
    return jnp.concatenate([strength] * (rows // strength.shape[0]), 0)


def current_kernel(
    order, back_order, shift, rows, strength, parts, less, great, less_out, great_out, wide, total, sems
):
    energies, _, row_count, orbitals = rows.shape
    block_count = total.shape[1]
    pad = energies // 2
    edge = jnp.zeros((pad, 2, row_count, orbitals), jnp.float32)
    wide[0:pad] = edge
    wide[pad + energies :] = edge
    for spot, energy in enumerate(order):
        wide[pad + energy] = rows[spot].astype(jnp.float32)
    factor = spread(strength[...], row_count)
    scale = spread(strength[...] * (1.0 / orbitals), row_count)
    first, second = shift[0], shift[1]

    def step(energy, carry):
        here = energy + pad
        above, below = (
            [wide[here + first, kind] + wide[here + second, kind] for kind in range(2)],
            [wide[here - first, kind] + wide[here - second, kind] for kind in range(2)],
        )
        gain = (1.0 + phonon_occupation) * above[0] + phonon_occupation * below[0]
        loss = (1.0 + phonon_occupation) * below[1] + phonon_occupation * above[1]
        less[energy] = (factor * gain).astype(less.dtype)
        great[energy] = (factor * loss).astype(great.dtype)
        flow = (gain * wide[here, 1] - loss * wide[here, 0]) * scale
        total[energy] = jnp.sum(flow.reshape(block_count, -1, orbitals), axis=1)
        return carry

    lax.fori_loop(0, energies, step, 0, unroll=4)
    flat = lane_sums(total[...].reshape(energies * block_count, orbitals))
    for spot, energy in enumerate(back_order):
        parts[spot] = flat[:, energy * block_count : (energy + 1) * block_count]
    pl.when(has_time())(functools.partial(copy_out, less, great, less_out, great_out, sems))


def local(
    green_ret, prior_less, prior_great, coupling, phonon_coupling, phonon_shift, active_blocks
):
    _, block_count, orbitals, _ = green_ret.shape
    devices, places = lax.axis_size("energy"), lax.axis_size("space")
    row_count = orbitals // devices
    last = block_count - 1
    order, back_order = orders(devices)
    swap = places == 2
    if swap:
        edges = [lambda: last * (1 - lax.axis_index("space"))]
    elif places > 1:
        edges = [lambda: last, lambda: 0]
    else:
        edges = []
    arrays, shift, open_mask, packed = load(
        edges, (green_ret, prior_less, prior_great, coupling), active_blocks, phonon_shift
    )
    green, less, great, coupling = arrays
    if swap:
        halos = (lax.ppermute(packed[0], "space", [(0, 1), (1, 0)]),)
    else:
        halos = tuple(
            shifted(edge, "space", step) for edge, step in zip(packed, (1, -1), strict=False)
        )
    split = row_count % 8 == 0 and block_count % 2 == 0
    if split:
        out_shape = (devices, 2, block_count * row_count, orbitals)
    else:
        out_shape = (2, block_count, orbitals, orbitals)
    outer = sorted({0, 1, last - 1, last})
    store_order = order if split else None
    diagonals = held((block_count, orbitals), jnp.float32)
    source, outgoing, diagonal = pl.pallas_call(
        functools.partial(hop_kernel, outer, store_order),
        out_shape=(
            held((len(outer), 2 * orbitals, orbitals), jnp.float32),
            held(out_shape, jnp.bfloat16),
            diagonals,
        ),
        in_specs=[VMEM] * 5,
        out_specs=(VMEM, VMEM, VMEM),
        compiler_params=params(),
        cost_estimate=pl.CostEstimate(
            flops=20 * block_count * orbitals**3,
            bytes_accessed=8 * block_count * orbitals**2,
            transcendentals=0,
        ),
    )(green, less, great, coupling, open_mask)
    outgoing, diagonal = pl.pallas_call(
        functools.partial(green_kernel, swap, outer, store_order),
        out_shape=(held(out_shape, jnp.bfloat16), diagonals),
        in_specs=[VMEM] * (6 + len(halos)),
        out_specs=(VMEM, VMEM),
        input_output_aliases={4: 0},
        compiler_params=params(),
    )(green, coupling, open_mask, source, outgoing, diagonal, *halos)
    if not split:
        outgoing = outgoing.reshape(2, block_count, devices, row_count, orbitals)
        outgoing = jnp.stack([outgoing[:, :, device] for device in order])
        outgoing = outgoing.reshape(devices, 2, block_count * row_count, orbitals)
    rows = exchange(outgoing, order)
    sigma_shape = (devices, block_count * row_count, orbitals)
    kept, written = held(sigma_shape, jnp.bfloat16), pltpu.HBM(sigma_shape, jnp.bfloat16)
    parts, less, great, *sigmas = pl.pallas_call(
        functools.partial(current_kernel, order, back_order),
        out_shape=(held((devices, 1, block_count), jnp.float32), kept, kept, written, written),
        in_specs=[SMEM, VMEM, VMEM],
        out_specs=(VMEM, VMEM, VMEM, ANY, ANY),
        scratch_shapes=[
            pltpu.VMEM((2 * devices, *rows.shape[1:]), jnp.float32),
            pltpu.VMEM((devices, block_count, orbitals), jnp.float32),
            pltpu.SemaphoreType.DMA((2,)),
        ],
        compiler_params=params(),
    )(in_smem(shift), rows, phonon_coupling)
    parts = exchange(parts, back_order)
    sums = jax.ShapeDtypeStruct((1, block_count), jnp.float32)
    current, ldos, *sigmas = pl.pallas_call(
        totals_kernel,
        out_shape=(sums, sums, written, written),
        in_specs=[VMEM] * 4 + [ANY] * 2,
        out_specs=(VMEM, VMEM, ANY, ANY),
        scratch_shapes=[pltpu.SemaphoreType.DMA((2,))],
        input_output_aliases={4: 2, 5: 3},
        compiler_params=params(),
    )(parts, diagonal, less, great, *sigmas)
    sigma_l, sigma_g = [
        sigma.reshape(devices, block_count, row_count, orbitals) for sigma in sigmas
    ]
    return (sigma_l, sigma_g, current, ldos)


def solution(mesh):
    return jax.shard_map(
        local,
        mesh=mesh,
        in_specs=(
            P("energy", "space", None, None),
            P("energy", "space", None, None),
            P("energy", "space", None, None),
            P("space", None, None),
            P("energy", None),
            P(),
            P(),
        ),
        out_specs=(
            P(None, "space", "energy", None),
            P(None, "space", "energy", None),
            P("energy", "space"),
            P("energy", "space"),
        ),
        check_vma=False,
    )
```

```python
import functools

import jax
import jax.numpy as jnp
from jax import lax
from jax.experimental import pallas as pl
from jax.experimental.pallas import tpu as pltpu
from jax.sharding import PartitionSpec as P

phonon_occupation = 0.5

VMEM = pl.BlockSpec(memory_space=pltpu.VMEM)
SMEM = pl.BlockSpec(memory_space=pltpu.SMEM)
ANY = pl.BlockSpec(memory_space=pl.ANY)


def shifted(value, axis, steps):
    count = lax.axis_size(axis)
    initial, last = (max(0, -steps), min(count, count - steps))
    return lax.ppermute(value, axis, [(source, source + steps) for source in range(initial, last)])


def orders(count):
    def starting(root):
        return [root] + [index for index in range(count) if index != root]

    return starting(11 * count // 16), starting(count - 1)


def exchange(chunks, order):
    return lax.all_to_all(
        chunks, "energy", split_axis=0, concat_axis=0, tiled=True, axis_index_groups=[order]
    )


def params():
    return pltpu.CompilerParams(vmem_limit_bytes=24 * 1024 * 1024)


def product(left, right):
    return jnp.dot(left, right, preferred_element_type=jnp.float32)


def product_t(left, right):
    return lax.dot_general(
        left, right, (((1,), (1,)), ((), ())), preferred_element_type=jnp.float32
    )


def held(shape, dtype):
    return pltpu.VMEM(shape, dtype)


def in_hbm(*arrays):
    return [pltpu.with_memory_space_constraint(array, pltpu.HBM) for array in arrays]


def in_smem(array):
    return pltpu.with_memory_space_constraint(array, pltpu.SMEM)


def load_kernel(edges, *refs):
    inputs, active, shift = refs[:4], refs[4], refs[5]
    outputs, steps, open_mask, wide = refs[6:10], refs[10], refs[11], refs[12]
    packed, counts, sems = refs[13 : 13 + len(edges)], refs[-2], refs[-1]
    blocks = [ref if ref.ndim == 3 else ref.at[0] for ref in inputs]
    pairs = [(active, counts), (shift, steps)]
    for block_of, target in zip(edges, packed):
        block = block_of()
        pairs += [(ref.at[block], target.at[slot]) for slot, ref in enumerate(blocks)]
    pairs += list(zip(blocks, outputs))
    copies = [
        pltpu.make_async_copy(origin, target, sems.at[index])
        for index, (origin, target) in enumerate(pairs)
    ]
    for copy in copies:
        copy.start()
    pad = wide.shape[0] // 4
    zeros = jnp.zeros((pad, *wide.shape[1:]), wide.dtype)
    wide[0:pad] = zeros
    wide[3 * pad :] = zeros
    for copy in copies:
        copy.wait()
    block_count = open_mask.shape[0]
    open_count = counts[lax.axis_index("energy")] - lax.axis_index("space") * block_count
    block_ids = lax.broadcasted_iota(jnp.int32, open_mask.shape, 0)
    open_mask[...] = (block_ids < open_count).astype(jnp.float32)


def load(edges, arrays, active, shift, devices):
    _, block_count, orbitals, _ = arrays[0].shape
    blocks = held((block_count, orbitals, orbitals), jnp.bfloat16)
    edge = held((len(arrays), orbitals, orbitals), jnp.bfloat16)
    copies = len(arrays) * (1 + len(edges)) + 2
    results = pl.pallas_call(
        functools.partial(load_kernel, edges),
        out_shape=(
            *[blocks] * len(arrays),
            pltpu.SMEM(shift.shape, shift.dtype),
            held((block_count, orbitals), jnp.float32),
            held((2 * devices, 2, block_count * orbitals // devices, orbitals), jnp.float32),
            *[edge] * len(edges),
        ),
        in_specs=[ANY] * (len(arrays) + 2),
        out_specs=(*[VMEM] * len(arrays), SMEM, VMEM, VMEM, *[VMEM] * len(edges)),
        scratch_shapes=[
            pltpu.SMEM(active.shape, active.dtype),
            pltpu.SemaphoreType.DMA((copies,)),
        ],
        compiler_params=params(),
    )(*in_hbm(*arrays, active, shift))
    kept = len(arrays)
    return results[:kept], results[kept : kept + 3], results[kept + 3 :]


def through(operator, less, great):
    rows = operator.shape[0]
    half = product(operator, jnp.concatenate([less, great], 1)).astype(jnp.bfloat16)
    stacked = jnp.concatenate([half[:, :rows], half[:, rows:]], 0)
    return product_t(stacked, operator)


def sandwiches(middles, green):
    orbitals = green.shape[1]
    halves, results = [], []
    for block, middle in enumerate(middles):
        middle = middle.astype(jnp.bfloat16)
        middle = jnp.concatenate([middle[:orbitals], middle[orbitals:]], 1)
        halves.append(product(green[block], middle).astype(jnp.bfloat16))
    for block, half in enumerate(halves):
        stacked = jnp.concatenate([half[:, :orbitals], half[:, orbitals:]], 0)
        results.append(product_t(stacked, green[block]))
    return results


def store(blocks, results, open_mask, outgoing, diagonal, order):
    orbitals = open_mask.shape[1]
    row_ids = lax.broadcasted_iota(jnp.int32, (orbitals, orbitals), 0)
    on_diagonal = row_ids == lax.broadcasted_iota(jnp.int32, (orbitals, orbitals), 1)
    kinds = {}
    for block in blocks:
        result = results[block] * open_mask[block : block + 1]
        kinds[block] = [result[:orbitals], result[orbitals:]]
        diagonal[block : block + 1] = jnp.sum(
            jnp.where(on_diagonal, kinds[block][0] + kinds[block][1], 0.0), axis=0, keepdims=True
        )
    for block in blocks:
        for kind in range(2):
            if order is None:
                outgoing[kind, block] = kinds[block][kind].astype(jnp.bfloat16)
            elif block % 2 == 0:
                rows = orbitals // len(order)
                for spot, device in enumerate(order):
                    piece = slice(device * rows, (device + 1) * rows)
                    pair = [kinds[block + step][kind][piece] for step in range(2)]
                    outgoing[spot, kind, block * rows : (block + 2) * rows] = jnp.concatenate(
                        pair, 0
                    ).astype(jnp.bfloat16)


def hop_kernel(outer, order, green, less, great, coupling, open_mask, partial, outgoing, diagonal):
    block_count, orbitals = green.shape[0], green.shape[1]
    blocks = range(block_count)
    hops, both, middles = [], [], []
    for block in blocks:
        factors = []
        if block + 1 < block_count:
            factors.append(coupling[block].T)
        if block > 0:
            factors.append(coupling[block - 1])
        hops.append(product(jnp.concatenate(factors, 0), green[block]).astype(jnp.bfloat16))
    for block in blocks:
        prior = jnp.concatenate([less[block], great[block]], 1)
        both.append(product(hops[block], prior).astype(jnp.bfloat16))
        middles.append(jnp.concatenate([less[block], great[block]], 0).astype(jnp.float32))
    for block in blocks:
        sent = []
        if block > 0:
            sent.append((block - 1, slice(0, orbitals)))
        if block + 1 < block_count:
            first = orbitals if block + 2 < block_count else 0
            sent.append((block + 1, slice(first, first + orbitals)))
        stacked = [
            jnp.concatenate([both[origin][piece, kind] for origin, piece in sent], 1)
            for kind in (slice(0, orbitals), slice(orbitals, 2 * orbitals))
        ]
        operators = jnp.concatenate([hops[origin][piece] for origin, piece in sent], 1)
        middles[block] = middles[block] + product_t(jnp.concatenate(stacked, 0), operators)
    results = sandwiches(middles, green)
    for slot, block in enumerate(outer):
        partial[slot] = results[block]
    inner = [block for block in blocks if block not in outer]
    store(inner, results, open_mask, outgoing, diagonal, order)


def edge_kernel(swap, outer, order, green, coupling, open_mask, partial, *rest):
    (_, inner_diagonal), halos, (outgoing, diagonal) = rest[:2], rest[2:-2], rest[-2:]
    last = green.shape[0] - 1
    place = lax.axis_index("space")
    results = {block: partial[slot] for slot, block in enumerate(outer)}

    def sent(retarded, hop, halo):
        operator = product(retarded, hop).astype(jnp.bfloat16)
        operator = product(operator, halo[0]).astype(jnp.bfloat16)
        return through(operator, halo[1], halo[2])

    if swap:
        (halo,) = halos
        retarded = jnp.where(place == 0, green[last], green[0])
        edge = sent(retarded, jnp.where(place == 0, coupling[last], halo[3].T), halo)
        results[0] = results[0] + jnp.where(place > 0, edge, 0.0)
        results[last] = results[last] + jnp.where(place == 0, edge, 0.0)
    elif halos:
        before, after = halos
        results[0] = results[0] + sent(green[0], before[3].T, before)
        results[last] = results[last] + sent(green[last], coupling[last], after)
    diagonal[...] = inner_diagonal[...]
    store(outer, results, open_mask, outgoing, diagonal, order)


def lane_sums(values):
    coarse = values.astype(jnp.bfloat16)
    fine = (values - coarse.astype(jnp.float32)).astype(jnp.bfloat16)
    ones = jnp.ones((8, 2 * values.shape[1]), jnp.bfloat16)
    return product_t(ones, jnp.concatenate([coarse, fine], 1))[0:1]


def copy_out(less, great, less_out, great_out, sems):
    copies = [
        pltpu.make_async_copy(less, less_out, sems.at[0]),
        pltpu.make_async_copy(great, great_out, sems.at[1]),
    ]
    for copy in copies:
        copy.start()
    for copy in copies:
        copy.wait()


def has_time():
    return lax.axis_index("energy") == 0


def totals_kernel(parts, diagonal, less, great, _, __, current, density, *outputs):
    total = parts[0]
    for spot in range(1, parts.shape[0]):
        total = total + parts[spot]
    current[...] = total
    density[...] = lane_sums(diagonal[...]) / diagonal.shape[1]
    pl.when(jnp.logical_not(has_time()))(functools.partial(copy_out, less, great, *outputs))


def spread(strength, rows):
    return jnp.concatenate([strength] * (rows // strength.shape[0]), 0)


def current_kernel(
    order, back_order, shift, rows, strength, _, parts, less, great, wide, *rest
):
    less_out, great_out, total, sems = rest
    energies, _, row_count, orbitals = rows.shape
    block_count = total.shape[1]
    pad = energies // 2
    for spot, energy in enumerate(order):
        wide[pad + energy] = rows[spot].astype(jnp.float32)
    factor = spread(strength[...], row_count)
    scale = spread(strength[...] * (1.0 / orbitals), row_count)
    first, second = shift[0], shift[1]

    def step(energy, carry):
        here = energy + pad
        above, below = (
            [wide[here + first, kind] + wide[here + second, kind] for kind in range(2)],
            [wide[here - first, kind] + wide[here - second, kind] for kind in range(2)],
        )
        gain = (1.0 + phonon_occupation) * above[0] + phonon_occupation * below[0]
        loss = (1.0 + phonon_occupation) * below[1] + phonon_occupation * above[1]
        less[energy] = (factor * gain).astype(less.dtype)
        great[energy] = (factor * loss).astype(great.dtype)
        flow = (gain * wide[here, 1] - loss * wide[here, 0]) * scale
        total[energy] = jnp.sum(flow.reshape(block_count, -1, orbitals), axis=1)
        return carry

    lax.fori_loop(0, energies, step, 0, unroll=4)
    flat = lane_sums(total[...].reshape(energies * block_count, orbitals))
    for spot, energy in enumerate(back_order):
        parts[spot] = flat[:, energy * block_count : (energy + 1) * block_count]
    pl.when(has_time())(functools.partial(copy_out, less, great, less_out, great_out, sems))


def local(
    green_ret, prior_less, prior_great, coupling, phonon_coupling, phonon_shift, active_blocks
):
    _, block_count, orbitals, _ = green_ret.shape
    devices, places = lax.axis_size("energy"), lax.axis_size("space")
    row_count = orbitals // devices
    last = block_count - 1
    order, back_order = orders(devices)
    swap = places == 2
    if swap:
        edges = [lambda: last * (1 - lax.axis_index("space"))]
    elif places > 1:
        edges = [lambda: last, lambda: 0]
    else:
        edges = []
    arrays, (shift, open_mask, wide), packed = load(
        edges,
        (green_ret, prior_less, prior_great, coupling),
        active_blocks,
        phonon_shift,
        devices,
    )
    green, less, great, coupling = arrays
    if swap:
        halos = (lax.ppermute(packed[0], "space", [(0, 1), (1, 0)]),)
    else:
        halos = tuple(
            shifted(edge, "space", step) for edge, step in zip(packed, (1, -1), strict=False)
        )
    split = row_count % 8 == 0 and block_count % 2 == 0
    if split:
        out_shape = (devices, 2, block_count * row_count, orbitals)
    else:
        out_shape = (2, block_count, orbitals, orbitals)
    outer = sorted({0, 1, last - 1, last})
    store_order = order if split else None
    diagonals = held((block_count, orbitals), jnp.float32)
    partial, outgoing, diagonal = pl.pallas_call(
        functools.partial(hop_kernel, outer, store_order),
        out_shape=(
            held((len(outer), 2 * orbitals, orbitals), jnp.float32),
            held(out_shape, jnp.bfloat16),
            diagonals,
        ),
        in_specs=[VMEM] * 5,
        out_specs=(VMEM, VMEM, VMEM),
        compiler_params=params(),
        cost_estimate=pl.CostEstimate(
            flops=20 * block_count * orbitals**3,
            bytes_accessed=8 * block_count * orbitals**2,
            transcendentals=0,
        ),
    )(green, less, great, coupling, open_mask)
    outgoing, diagonal = pl.pallas_call(
        functools.partial(edge_kernel, swap, outer, store_order),
        out_shape=(held(out_shape, jnp.bfloat16), diagonals),
        in_specs=[VMEM] * (6 + len(halos)),
        out_specs=(VMEM, VMEM),
        input_output_aliases={4: 0},
        compiler_params=params(),
    )(green, coupling, open_mask, partial, outgoing, diagonal, *halos)
    if not split:
        outgoing = outgoing.reshape(2, block_count, devices, row_count, orbitals)
        outgoing = jnp.stack([outgoing[:, :, device] for device in order])
        outgoing = outgoing.reshape(devices, 2, block_count * row_count, orbitals)
    rows = exchange(outgoing, order)
    sigma_shape = (devices, block_count * row_count, orbitals)
    kept, written = held(sigma_shape, jnp.bfloat16), pltpu.HBM(sigma_shape, jnp.bfloat16)
    parts, less, great, _, *sigmas = pl.pallas_call(
        functools.partial(current_kernel, order, back_order),
        out_shape=(
            held((devices, 1, block_count), jnp.float32),
            kept,
            kept,
            held(wide.shape, wide.dtype),
            written,
            written,
        ),
        in_specs=[SMEM, VMEM, VMEM, VMEM],
        out_specs=(VMEM, VMEM, VMEM, VMEM, ANY, ANY),
        input_output_aliases={3: 3},
        scratch_shapes=[
            pltpu.VMEM((devices, block_count, orbitals), jnp.float32),
            pltpu.SemaphoreType.DMA((2,)),
        ],
        compiler_params=params(),
    )(in_smem(shift), rows, phonon_coupling, wide)
    parts = exchange(parts, back_order)
    sums = jax.ShapeDtypeStruct((1, block_count), jnp.float32)
    current, ldos, *sigmas = pl.pallas_call(
        totals_kernel,
        out_shape=(sums, sums, written, written),
        in_specs=[VMEM] * 4 + [ANY] * 2,
        out_specs=(VMEM, VMEM, ANY, ANY),
        scratch_shapes=[pltpu.SemaphoreType.DMA((2,))],
        input_output_aliases={4: 2, 5: 3},
        compiler_params=params(),
    )(parts, diagonal, less, great, *sigmas)
    sigma_l, sigma_g = [
        sigma.reshape(devices, block_count, row_count, orbitals) for sigma in sigmas
    ]
    return (sigma_l, sigma_g, current, ldos)


def solution(mesh):
    return jax.shard_map(
        local,
        mesh=mesh,
        in_specs=(
            P("energy", "space", None, None),
            P("energy", "space", None, None),
            P("energy", "space", None, None),
            P("space", None, None),
            P("energy", None),
            P(),
            P(),
        ),
        out_specs=(
            P(None, "space", "energy", None),
            P(None, "space", "energy", None),
            P("energy", "space"),
            P("energy", "space"),
        ),
        check_vma=False,
    )
```

```python
import functools

import jax
import jax.numpy as jnp
from jax import lax
from jax.experimental import pallas as pl
from jax.experimental.pallas import tpu as pltpu
from jax.sharding import PartitionSpec as P

phonon_occupation = 0.5

VMEM = pl.BlockSpec(memory_space=pltpu.VMEM)
SMEM = pl.BlockSpec(memory_space=pltpu.SMEM)
ANY = pl.BlockSpec(memory_space=pl.ANY)


def shifted(value, axis, steps):
    count = lax.axis_size(axis)
    initial, last = (max(0, -steps), min(count, count - steps))
    return lax.ppermute(value, axis, [(source, source + steps) for source in range(initial, last)])


def orders(count):
    def starting(root):
        return [root] + [index for index in range(count) if index != root]

    return starting(11 * count // 16), starting(count - 1)


def exchange(chunks, order):
    return lax.all_to_all(
        chunks, "energy", split_axis=0, concat_axis=0, tiled=True, axis_index_groups=[order]
    )


def params():
    return pltpu.CompilerParams(vmem_limit_bytes=24 * 1024 * 1024)


def product(left, right):
    return jnp.dot(left, right, preferred_element_type=jnp.float32)


def product_t(left, right):
    return lax.dot_general(
        left, right, (((1,), (1,)), ((), ())), preferred_element_type=jnp.float32
    )


def held(shape, dtype):
    return pltpu.VMEM(shape, dtype)


def in_hbm(*arrays):
    return [pltpu.with_memory_space_constraint(array, pltpu.HBM) for array in arrays]


def in_smem(array):
    return pltpu.with_memory_space_constraint(array, pltpu.SMEM)


def load_kernel(edges, *refs):
    inputs, active, shift = refs[:4], refs[4], refs[5]
    outputs, steps, open_mask, wide = refs[6:10], refs[10], refs[11], refs[12]
    packed, counts, sems = refs[13 : 13 + len(edges)], refs[-2], refs[-1]
    blocks = [ref if ref.ndim == 3 else ref.at[0] for ref in inputs]
    pairs = [(active, counts), (shift, steps)]
    for block_of, target in zip(edges, packed):
        block = block_of()
        pairs += [(ref.at[block], target.at[slot]) for slot, ref in enumerate(blocks)]
    pairs += list(zip(blocks, outputs))
    copies = [
        pltpu.make_async_copy(origin, target, sems.at[index])
        for index, (origin, target) in enumerate(pairs)
    ]
    for copy in copies:
        copy.start()
    pad = wide.shape[0] // 4
    zeros = jnp.zeros((pad, *wide.shape[1:]), wide.dtype)
    wide[0:pad] = zeros
    wide[3 * pad :] = zeros
    for copy in copies:
        copy.wait()
    block_count = open_mask.shape[0]
    open_count = counts[lax.axis_index("energy")] - lax.axis_index("space") * block_count
    block_ids = lax.broadcasted_iota(jnp.int32, open_mask.shape, 0)
    open_mask[...] = (block_ids < open_count).astype(jnp.float32)


def load(edges, arrays, active, shift, devices):
    _, block_count, orbitals, _ = arrays[0].shape
    blocks = held((block_count, orbitals, orbitals), jnp.bfloat16)
    edge = held((len(arrays), orbitals, orbitals), jnp.bfloat16)
    copies = len(arrays) * (1 + len(edges)) + 2
    results = pl.pallas_call(
        functools.partial(load_kernel, edges),
        out_shape=(
            *[blocks] * len(arrays),
            pltpu.SMEM(shift.shape, shift.dtype),
            held((block_count, orbitals), jnp.float32),
            held((2 * devices, 2, block_count * orbitals // devices, orbitals), jnp.float32),
            *[edge] * len(edges),
        ),
        in_specs=[ANY] * (len(arrays) + 2),
        out_specs=(*[VMEM] * len(arrays), SMEM, VMEM, VMEM, *[VMEM] * len(edges)),
        scratch_shapes=[
            pltpu.SMEM(active.shape, active.dtype),
            pltpu.SemaphoreType.DMA((copies,)),
        ],
        compiler_params=params(),
    )(*in_hbm(*arrays, active, shift))
    kept = len(arrays)
    return results[:kept], results[kept : kept + 3], results[kept + 3 :]


def through(operator, less, great):
    rows = operator.shape[0]
    half = product(operator, jnp.concatenate([less, great], 1)).astype(jnp.bfloat16)
    stacked = jnp.concatenate([half[:, :rows], half[:, rows:]], 0)
    return product_t(stacked, operator)


def sandwiches(middles, green):
    orbitals = green.shape[1]
    halves, results = [], []
    for block, middle in enumerate(middles):
        middle = middle.astype(jnp.bfloat16)
        middle = jnp.concatenate([middle[:orbitals], middle[orbitals:]], 1)
        halves.append(product(green[block], middle).astype(jnp.bfloat16))
    for block, half in enumerate(halves):
        stacked = jnp.concatenate([half[:, :orbitals], half[:, orbitals:]], 0)
        results.append(product_t(stacked, green[block]))
    return results


def store(blocks, results, open_mask, outgoing, diagonal, order):
    orbitals = open_mask.shape[1]
    row_ids = lax.broadcasted_iota(jnp.int32, (orbitals, orbitals), 0)
    on_diagonal = row_ids == lax.broadcasted_iota(jnp.int32, (orbitals, orbitals), 1)
    kinds = {}
    for block in blocks:
        result = results[block] * open_mask[block : block + 1]
        kinds[block] = [result[:orbitals], result[orbitals:]]
        diagonal[block : block + 1] = jnp.sum(
            jnp.where(on_diagonal, kinds[block][0] + kinds[block][1], 0.0), axis=0, keepdims=True
        )
    for block in blocks:
        for kind in range(2):
            if order is None:
                outgoing[kind, block] = kinds[block][kind].astype(jnp.bfloat16)
            elif block % 2 == 0:
                rows = orbitals // len(order)
                for spot, device in enumerate(order):
                    piece = slice(device * rows, (device + 1) * rows)
                    pair = [kinds[block + step][kind][piece] for step in range(2)]
                    outgoing[spot, kind, block * rows : (block + 2) * rows] = jnp.concatenate(
                        pair, 0
                    ).astype(jnp.bfloat16)


def hop_kernel(outer, order, green, less, great, coupling, open_mask, partial, outgoing, diagonal):
    block_count, orbitals = green.shape[0], green.shape[1]
    blocks = range(block_count)
    hops, both, middles = [], [], []
    for block in blocks:
        factors = []
        if block + 1 < block_count:
            factors.append(coupling[block].T)
        if block > 0:
            factors.append(coupling[block - 1])
        hops.append(product(jnp.concatenate(factors, 0), green[block]).astype(jnp.bfloat16))
    for block in blocks:
        prior = jnp.concatenate([less[block], great[block]], 1)
        both.append(product(hops[block], prior).astype(jnp.bfloat16))
        middles.append(jnp.concatenate([less[block], great[block]], 0).astype(jnp.float32))
    for block in blocks:
        sent = []
        if block > 0:
            sent.append((block - 1, slice(0, orbitals)))
        if block + 1 < block_count:
            first = orbitals if block + 2 < block_count else 0
            sent.append((block + 1, slice(first, first + orbitals)))
        stacked = [
            jnp.concatenate([both[origin][piece, kind] for origin, piece in sent], 1)
            for kind in (slice(0, orbitals), slice(orbitals, 2 * orbitals))
        ]
        operators = jnp.concatenate([hops[origin][piece] for origin, piece in sent], 1)
        middles[block] = middles[block] + product_t(jnp.concatenate(stacked, 0), operators)
    results = sandwiches(middles, green)
    for slot, block in enumerate(outer):
        partial[slot] = results[block]
    inner = [block for block in blocks if block not in outer]
    store(inner, results, open_mask, outgoing, diagonal, order)


def edge_kernel(swap, outer, order, green, coupling, open_mask, partial, *rest):
    (_, inner_diagonal), halos, (outgoing, diagonal) = rest[:2], rest[2:-2], rest[-2:]
    last = green.shape[0] - 1
    place = lax.axis_index("space")
    results = {block: partial[slot] for slot, block in enumerate(outer)}

    def sent(retarded, hop, halo):
        operator = product(retarded, hop).astype(jnp.bfloat16)
        operator = product(operator, halo[0]).astype(jnp.bfloat16)
        return through(operator, halo[1], halo[2])

    if swap:
        (halo,) = halos
        retarded = jnp.where(place == 0, green[last], green[0])
        edge = sent(retarded, jnp.where(place == 0, coupling[last], halo[3].T), halo)
        results[0] = results[0] + jnp.where(place > 0, edge, 0.0)
        results[last] = results[last] + jnp.where(place == 0, edge, 0.0)
    elif halos:
        before, after = halos
        results[0] = results[0] + sent(green[0], before[3].T, before)
        results[last] = results[last] + sent(green[last], coupling[last], after)
    diagonal[...] = inner_diagonal[...]
    store(outer, results, open_mask, outgoing, diagonal, order)


def lane_sums(values):
    coarse = values.astype(jnp.bfloat16)
    fine = (values - coarse.astype(jnp.float32)).astype(jnp.bfloat16)
    ones = jnp.ones((8, 2 * values.shape[1]), jnp.bfloat16)
    return product_t(ones, jnp.concatenate([coarse, fine], 1))[0:1]


def totals_kernel(
    parts, diagonal, less, great, current_out, density_out, less_out, great_out, current, density, sems
):
    pairs = (
        (less, less_out),
        (great, great_out),
        (density, density_out),
        (current, current_out),
    )
    copies = [
        pltpu.make_async_copy(origin, target, sems.at[index])
        for index, (origin, target) in enumerate(pairs)
    ]
    total = parts[0]
    for spot in range(1, parts.shape[0]):
        total = total + parts[spot]
    current[...] = total
    copies[3].start()
    copies[0].start()
    copies[1].start()
    density[...] = lane_sums(diagonal[...]) / diagonal.shape[1]
    copies[2].start()
    for copy in copies:
        copy.wait()


def spread(strength, rows):
    return jnp.concatenate([strength] * (rows // strength.shape[0]), 0)


def current_kernel(
    order, back_order, shift, rows, strength, _, parts, less, great, wide, total
):
    energies, _, row_count, orbitals = rows.shape
    block_count = total.shape[1]
    pad = energies // 2
    for spot, energy in enumerate(order):
        wide[pad + energy] = rows[spot].astype(jnp.float32)
    factor = spread(strength[...], row_count)
    scale = spread(strength[...] * (1.0 / orbitals), row_count)
    first, second = shift[0], shift[1]

    def step(energy, carry):
        here = energy + pad
        above, below = (
            [wide[here + first, kind] + wide[here + second, kind] for kind in range(2)],
            [wide[here - first, kind] + wide[here - second, kind] for kind in range(2)],
        )
        gain = (1.0 + phonon_occupation) * above[0] + phonon_occupation * below[0]
        loss = (1.0 + phonon_occupation) * below[1] + phonon_occupation * above[1]
        less[energy] = (factor * gain).astype(less.dtype)
        great[energy] = (factor * loss).astype(great.dtype)
        flow = (gain * wide[here, 1] - loss * wide[here, 0]) * scale
        total[energy] = jnp.sum(flow.reshape(block_count, -1, orbitals), axis=1)
        return carry

    lax.fori_loop(0, energies, step, 0, unroll=4)
    flat = lane_sums(total[...].reshape(energies * block_count, orbitals))
    for spot, energy in enumerate(back_order):
        parts[spot] = flat[:, energy * block_count : (energy + 1) * block_count]


def local(
    green_ret, prior_less, prior_great, coupling, phonon_coupling, phonon_shift, active_blocks
):
    _, block_count, orbitals, _ = green_ret.shape
    devices, places = lax.axis_size("energy"), lax.axis_size("space")
    row_count = orbitals // devices
    last = block_count - 1
    order, back_order = orders(devices)
    swap = places == 2
    if swap:
        edges = [lambda: last * (1 - lax.axis_index("space"))]
    elif places > 1:
        edges = [lambda: last, lambda: 0]
    else:
        edges = []
    arrays, (shift, open_mask, wide), packed = load(
        edges,
        (green_ret, prior_less, prior_great, coupling),
        active_blocks,
        phonon_shift,
        devices,
    )
    green, less, great, coupling = arrays
    if swap:
        halos = (lax.ppermute(packed[0], "space", [(0, 1), (1, 0)]),)
    else:
        halos = tuple(
            shifted(edge, "space", step) for edge, step in zip(packed, (1, -1), strict=False)
        )
    split = row_count % 8 == 0 and block_count % 2 == 0
    if split:
        out_shape = (devices, 2, block_count * row_count, orbitals)
    else:
        out_shape = (2, block_count, orbitals, orbitals)
    outer = sorted({0, 1, last - 1, last})
    store_order = order if split else None
    diagonals = held((block_count, orbitals), jnp.float32)
    partial, outgoing, diagonal = pl.pallas_call(
        functools.partial(hop_kernel, outer, store_order),
        out_shape=(
            held((len(outer), 2 * orbitals, orbitals), jnp.float32),
            held(out_shape, jnp.bfloat16),
            diagonals,
        ),
        in_specs=[VMEM] * 5,
        out_specs=(VMEM, VMEM, VMEM),
        compiler_params=params(),
        cost_estimate=pl.CostEstimate(
            flops=20 * block_count * orbitals**3,
            bytes_accessed=8 * block_count * orbitals**2,
            transcendentals=0,
        ),
    )(green, less, great, coupling, open_mask)
    outgoing, diagonal = pl.pallas_call(
        functools.partial(edge_kernel, swap, outer, store_order),
        out_shape=(held(out_shape, jnp.bfloat16), diagonals),
        in_specs=[VMEM] * (6 + len(halos)),
        out_specs=(VMEM, VMEM),
        input_output_aliases={4: 0},
        compiler_params=params(),
    )(green, coupling, open_mask, partial, outgoing, diagonal, *halos)
    if not split:
        outgoing = outgoing.reshape(2, block_count, devices, row_count, orbitals)
        outgoing = jnp.stack([outgoing[:, :, device] for device in order])
        outgoing = outgoing.reshape(devices, 2, block_count * row_count, orbitals)
    rows = exchange(outgoing, order)
    sigma_shape = (devices, block_count * row_count, orbitals)
    kept, written = held(sigma_shape, jnp.bfloat16), pltpu.HBM(sigma_shape, jnp.bfloat16)
    parts, less, great, _ = pl.pallas_call(
        functools.partial(current_kernel, order, back_order),
        out_shape=(
            held((devices, 1, block_count), jnp.float32),
            kept,
            kept,
            held(wide.shape, wide.dtype),
        ),
        in_specs=[SMEM, VMEM, VMEM, VMEM],
        out_specs=(VMEM, VMEM, VMEM, VMEM),
        input_output_aliases={3: 3},
        scratch_shapes=[pltpu.VMEM((devices, block_count, orbitals), jnp.float32)],
        compiler_params=params(),
    )(in_smem(shift), rows, phonon_coupling, wide)
    parts = exchange(parts, back_order)
    sums = pltpu.HBM((1, block_count), jnp.float32)
    current, ldos, *sigmas = pl.pallas_call(
        totals_kernel,
        out_shape=(sums, sums, written, written),
        in_specs=[VMEM] * 4,
        out_specs=[ANY] * 4,
        scratch_shapes=[
            *[pltpu.VMEM((1, block_count), jnp.float32)] * 2,
            pltpu.SemaphoreType.DMA((4,)),
        ],
        compiler_params=params(),
    )(parts, diagonal, less, great)
    sigma_l, sigma_g = [
        sigma.reshape(devices, block_count, row_count, orbitals) for sigma in sigmas
    ]
    return (sigma_l, sigma_g, current, ldos)


def solution(mesh):
    return jax.shard_map(
        local,
        mesh=mesh,
        in_specs=(
            P("energy", "space", None, None),
            P("energy", "space", None, None),
            P("energy", "space", None, None),
            P("space", None, None),
            P("energy", None),
            P(),
            P(),
        ),
        out_specs=(
            P(None, "space", "energy", None),
            P(None, "space", "energy", None),
            P("energy", "space"),
            P("energy", "space"),
        ),
        check_vma=False,
    )
```

```python
import functools

import jax
import jax.numpy as jnp
from jax import lax
from jax.experimental import pallas as pl
from jax.experimental.pallas import tpu as pltpu
from jax.sharding import PartitionSpec as P

phonon_occupation = 0.5

VMEM = pl.BlockSpec(memory_space=pltpu.VMEM)
SMEM = pl.BlockSpec(memory_space=pltpu.SMEM)
ANY = pl.BlockSpec(memory_space=pl.ANY)


def shifted(value, axis, steps):
    count = lax.axis_size(axis)
    initial, last = (max(0, -steps), min(count, count - steps))
    return lax.ppermute(value, axis, [(source, source + steps) for source in range(initial, last)])


def orders(count):
    def starting(root):
        return [root] + [index for index in range(count) if index != root]

    return starting(11 * count // 16), starting(count - 1)


def exchange(chunks, order):
    return lax.all_to_all(
        chunks, "energy", split_axis=0, concat_axis=0, tiled=True, axis_index_groups=[order]
    )


def params():
    return pltpu.CompilerParams(vmem_limit_bytes=24 * 1024 * 1024)


def product(left, right):
    return jnp.dot(left, right, preferred_element_type=jnp.float32)


def product_t(left, right):
    return lax.dot_general(
        left, right, (((1,), (1,)), ((), ())), preferred_element_type=jnp.float32
    )


def held(shape, dtype):
    return pltpu.VMEM(shape, dtype)


def in_hbm(*arrays):
    return [pltpu.with_memory_space_constraint(array, pltpu.HBM) for array in arrays]


def in_smem(array):
    return pltpu.with_memory_space_constraint(array, pltpu.SMEM)


def load_kernel(edges, *refs):
    inputs, active, shift = refs[:4], refs[4], refs[5]
    outputs, steps, open_mask, wide = refs[6:10], refs[10], refs[11], refs[12]
    packed, counts, sems = refs[13 : 13 + len(edges)], refs[-2], refs[-1]
    blocks = [ref if ref.ndim == 3 else ref.at[0] for ref in inputs]
    pairs = [(active, counts), (shift, steps)]
    for block_of, target in zip(edges, packed):
        block = block_of()
        pairs += [(ref.at[block], target.at[slot]) for slot, ref in enumerate(blocks)]
    pairs += list(zip(blocks, outputs))
    copies = [
        pltpu.make_async_copy(origin, target, sems.at[index])
        for index, (origin, target) in enumerate(pairs)
    ]
    for copy in copies:
        copy.start()
    pad = wide.shape[0] // 4
    zeros = jnp.zeros((pad, *wide.shape[1:]), wide.dtype)
    wide[0:pad] = zeros
    wide[3 * pad :] = zeros
    for copy in copies:
        copy.wait()
    block_count = open_mask.shape[0]
    open_count = counts[lax.axis_index("energy")] - lax.axis_index("space") * block_count
    block_ids = lax.broadcasted_iota(jnp.int32, open_mask.shape, 0)
    open_mask[...] = (block_ids < open_count).astype(jnp.float32)


def load(edges, arrays, active, shift, devices):
    _, block_count, orbitals, _ = arrays[0].shape
    blocks = held((block_count, orbitals, orbitals), jnp.bfloat16)
    edge = held((len(arrays), orbitals, orbitals), jnp.bfloat16)
    copies = len(arrays) * (1 + len(edges)) + 2
    results = pl.pallas_call(
        functools.partial(load_kernel, edges),
        out_shape=(
            *[blocks] * len(arrays),
            pltpu.SMEM(shift.shape, shift.dtype),
            held((block_count, orbitals), jnp.float32),
            held((2 * devices, 2, block_count * orbitals // devices, orbitals), jnp.float32),
            *[edge] * len(edges),
        ),
        in_specs=[ANY] * (len(arrays) + 2),
        out_specs=(*[VMEM] * len(arrays), SMEM, VMEM, VMEM, *[VMEM] * len(edges)),
        scratch_shapes=[
            pltpu.SMEM(active.shape, active.dtype),
            pltpu.SemaphoreType.DMA((copies,)),
        ],
        compiler_params=params(),
    )(*in_hbm(*arrays, active, shift))
    kept = len(arrays)
    return results[:kept], results[kept : kept + 3], results[kept + 3 :]


def through(operator, less, great):
    rows = operator.shape[0]
    half = product(operator, jnp.concatenate([less, great], 1)).astype(jnp.bfloat16)
    stacked = jnp.concatenate([half[:, :rows], half[:, rows:]], 0)
    return product_t(stacked, operator)


def sandwiches(middles, green):
    orbitals = green.shape[1]
    halves, results = [], []
    for block, middle in enumerate(middles):
        middle = middle.astype(jnp.bfloat16)
        middle = jnp.concatenate([middle[:orbitals], middle[orbitals:]], 1)
        halves.append(product(green[block], middle).astype(jnp.bfloat16))
    for block, half in enumerate(halves):
        stacked = jnp.concatenate([half[:, :orbitals], half[:, orbitals:]], 0)
        results.append(product_t(stacked, green[block]))
    return results


def store(blocks, results, open_mask, outgoing, diagonal, order):
    orbitals = open_mask.shape[1]
    row_ids = lax.broadcasted_iota(jnp.int32, (orbitals, orbitals), 0)
    on_diagonal = row_ids == lax.broadcasted_iota(jnp.int32, (orbitals, orbitals), 1)
    kinds = {}
    for block in blocks:
        result = results[block] * open_mask[block : block + 1]
        kinds[block] = [result[:orbitals], result[orbitals:]]
        diagonal[block : block + 1] = jnp.sum(
            jnp.where(on_diagonal, kinds[block][0] + kinds[block][1], 0.0), axis=0, keepdims=True
        )
    for block in blocks:
        for kind in range(2):
            if order is None:
                outgoing[kind, block] = kinds[block][kind].astype(jnp.bfloat16)
            elif block % 2 == 0:
                rows = orbitals // len(order)
                for spot, device in enumerate(order):
                    piece = slice(device * rows, (device + 1) * rows)
                    pair = [kinds[block + step][kind][piece] for step in range(2)]
                    outgoing[spot, kind, block * rows : (block + 2) * rows] = jnp.concatenate(
                        pair, 0
                    ).astype(jnp.bfloat16)


def hop_kernel(outer, order, green, less, great, coupling, open_mask, partial, outgoing, diagonal):
    block_count, orbitals = green.shape[0], green.shape[1]
    blocks = range(block_count)
    hops, both, middles = [], [], []
    for block in blocks:
        factors = []
        if block + 1 < block_count:
            factors.append(coupling[block].T)
        if block > 0:
            factors.append(coupling[block - 1])
        hops.append(product(jnp.concatenate(factors, 0), green[block]).astype(jnp.bfloat16))
    for block in blocks:
        prior = jnp.concatenate([less[block], great[block]], 1)
        both.append(product(hops[block], prior).astype(jnp.bfloat16))
        middles.append(jnp.concatenate([less[block], great[block]], 0).astype(jnp.float32))
    for block in blocks:
        sent = []
        if block > 0:
            sent.append((block - 1, slice(0, orbitals)))
        if block + 1 < block_count:
            first = orbitals if block + 2 < block_count else 0
            sent.append((block + 1, slice(first, first + orbitals)))
        stacked = [
            jnp.concatenate([both[origin][piece, kind] for origin, piece in sent], 1)
            for kind in (slice(0, orbitals), slice(orbitals, 2 * orbitals))
        ]
        operators = jnp.concatenate([hops[origin][piece] for origin, piece in sent], 1)
        middles[block] = middles[block] + product_t(jnp.concatenate(stacked, 0), operators)
    results = sandwiches(middles, green)
    for slot, block in enumerate(outer):
        partial[slot] = results[block]
    inner = [block for block in blocks if block not in outer]
    store(inner, results, open_mask, outgoing, diagonal, order)


def edge_kernel(swap, outer, order, green, coupling, open_mask, partial, *rest):
    (_, inner_diagonal), halos, (outgoing, diagonal) = rest[:2], rest[2:-2], rest[-2:]
    last = green.shape[0] - 1
    place = lax.axis_index("space")
    results = {block: partial[slot] for slot, block in enumerate(outer)}

    def sent(retarded, hop, halo):
        operator = product(retarded, hop).astype(jnp.bfloat16)
        operator = product(operator, halo[0]).astype(jnp.bfloat16)
        return through(operator, halo[1], halo[2])

    if swap:
        (halo,) = halos
        retarded = jnp.where(place == 0, green[last], green[0])
        edge = sent(retarded, jnp.where(place == 0, coupling[last], halo[3].T), halo)
        results[0] = results[0] + jnp.where(place > 0, edge, 0.0)
        results[last] = results[last] + jnp.where(place == 0, edge, 0.0)
    elif halos:
        before, after = halos
        results[0] = results[0] + sent(green[0], before[3].T, before)
        results[last] = results[last] + sent(green[last], coupling[last], after)
    diagonal[...] = inner_diagonal[...]
    store(outer, results, open_mask, outgoing, diagonal, order)


def lane_sums(values):
    coarse = values.astype(jnp.bfloat16)
    fine = (values - coarse.astype(jnp.float32)).astype(jnp.bfloat16)
    ones = jnp.ones((8, 2 * values.shape[1]), jnp.bfloat16)
    return product_t(ones, jnp.concatenate([coarse, fine], 1))[0:1]


def copy_out(less, great, less_out, great_out, sems):
    copies = [
        pltpu.make_async_copy(less, less_out, sems.at[0]),
        pltpu.make_async_copy(great, great_out, sems.at[1]),
    ]
    for copy in copies:
        copy.start()
    for copy in copies:
        copy.wait()


def has_time():
    return lax.axis_index("energy") == 0


def totals_kernel(
    parts, diagonal, less, great, _, __, current_out, density_out, less_out, great_out, *scratch
):
    current, density, sums_sems, sems = scratch
    total = parts[0]
    for spot in range(1, parts.shape[0]):
        total = total + parts[spot]
    current[...] = total
    first = pltpu.make_async_copy(current, current_out, sums_sems.at[0])
    first.start()
    density[...] = lane_sums(diagonal[...]) / diagonal.shape[1]
    second = pltpu.make_async_copy(density, density_out, sums_sems.at[1])
    second.start()
    pl.when(jnp.logical_not(has_time()))(
        functools.partial(copy_out, less, great, less_out, great_out, sems)
    )
    first.wait()
    second.wait()


def spread(strength, rows):
    return jnp.concatenate([strength] * (rows // strength.shape[0]), 0)


def current_kernel(
    order, back_order, shift, rows, strength, _, parts, less, great, wide, *rest
):
    less_out, great_out, total, sems = rest
    energies, _, row_count, orbitals = rows.shape
    block_count = total.shape[1]
    pad = energies // 2
    for spot, energy in enumerate(order):
        wide[pad + energy] = rows[spot].astype(jnp.float32)
    factor = spread(strength[...], row_count)
    scale = spread(strength[...] * (1.0 / orbitals), row_count)
    first, second = shift[0], shift[1]

    def step(energy, carry):
        here = energy + pad
        above, below = (
            [wide[here + first, kind] + wide[here + second, kind] for kind in range(2)],
            [wide[here - first, kind] + wide[here - second, kind] for kind in range(2)],
        )
        gain = (1.0 + phonon_occupation) * above[0] + phonon_occupation * below[0]
        loss = (1.0 + phonon_occupation) * below[1] + phonon_occupation * above[1]
        less[energy] = (factor * gain).astype(less.dtype)
        great[energy] = (factor * loss).astype(great.dtype)
        flow = (gain * wide[here, 1] - loss * wide[here, 0]) * scale
        total[energy] = jnp.sum(flow.reshape(block_count, -1, orbitals), axis=1)
        return carry

    lax.fori_loop(0, energies, step, 0, unroll=4)
    flat = lane_sums(total[...].reshape(energies * block_count, orbitals))
    for spot, energy in enumerate(back_order):
        parts[spot] = flat[:, energy * block_count : (energy + 1) * block_count]
    pl.when(has_time())(functools.partial(copy_out, less, great, less_out, great_out, sems))


def local(
    green_ret, prior_less, prior_great, coupling, phonon_coupling, phonon_shift, active_blocks
):
    _, block_count, orbitals, _ = green_ret.shape
    devices, places = lax.axis_size("energy"), lax.axis_size("space")
    row_count = orbitals // devices
    last = block_count - 1
    order, back_order = orders(devices)
    swap = places == 2
    if swap:
        edges = [lambda: last * (1 - lax.axis_index("space"))]
    elif places > 1:
        edges = [lambda: last, lambda: 0]
    else:
        edges = []
    arrays, (shift, open_mask, wide), packed = load(
        edges,
        (green_ret, prior_less, prior_great, coupling),
        active_blocks,
        phonon_shift,
        devices,
    )
    green, less, great, coupling = arrays
    if swap:
        halos = (lax.ppermute(packed[0], "space", [(0, 1), (1, 0)]),)
    else:
        halos = tuple(
            shifted(edge, "space", step) for edge, step in zip(packed, (1, -1), strict=False)
        )
    split = row_count % 8 == 0 and block_count % 2 == 0
    if split:
        out_shape = (devices, 2, block_count * row_count, orbitals)
    else:
        out_shape = (2, block_count, orbitals, orbitals)
    outer = sorted({0, 1, last - 1, last})
    store_order = order if split else None
    diagonals = held((block_count, orbitals), jnp.float32)
    partial, outgoing, diagonal = pl.pallas_call(
        functools.partial(hop_kernel, outer, store_order),
        out_shape=(
            held((len(outer), 2 * orbitals, orbitals), jnp.float32),
            held(out_shape, jnp.bfloat16),
            diagonals,
        ),
        in_specs=[VMEM] * 5,
        out_specs=(VMEM, VMEM, VMEM),
        compiler_params=params(),
        cost_estimate=pl.CostEstimate(
            flops=20 * block_count * orbitals**3,
            bytes_accessed=8 * block_count * orbitals**2,
            transcendentals=0,
        ),
    )(green, less, great, coupling, open_mask)
    outgoing, diagonal = pl.pallas_call(
        functools.partial(edge_kernel, swap, outer, store_order),
        out_shape=(held(out_shape, jnp.bfloat16), diagonals),
        in_specs=[VMEM] * (6 + len(halos)),
        out_specs=(VMEM, VMEM),
        input_output_aliases={4: 0},
        compiler_params=params(),
    )(green, coupling, open_mask, partial, outgoing, diagonal, *halos)
    if not split:
        outgoing = outgoing.reshape(2, block_count, devices, row_count, orbitals)
        outgoing = jnp.stack([outgoing[:, :, device] for device in order])
        outgoing = outgoing.reshape(devices, 2, block_count * row_count, orbitals)
    rows = exchange(outgoing, order)
    sigma_shape = (devices, block_count * row_count, orbitals)
    kept, written = held(sigma_shape, jnp.bfloat16), pltpu.HBM(sigma_shape, jnp.bfloat16)
    parts, less, great, _, *sigmas = pl.pallas_call(
        functools.partial(current_kernel, order, back_order),
        out_shape=(
            held((devices, 1, block_count), jnp.float32),
            kept,
            kept,
            held(wide.shape, wide.dtype),
            written,
            written,
        ),
        in_specs=[SMEM, VMEM, VMEM, VMEM],
        out_specs=(VMEM, VMEM, VMEM, VMEM, ANY, ANY),
        input_output_aliases={3: 3},
        scratch_shapes=[
            pltpu.VMEM((devices, block_count, orbitals), jnp.float32),
            pltpu.SemaphoreType.DMA((2,)),
        ],
        compiler_params=params(),
    )(in_smem(shift), rows, phonon_coupling, wide)
    parts = exchange(parts, back_order)
    sums = pltpu.HBM((1, block_count), jnp.float32)
    current, ldos, *sigmas = pl.pallas_call(
        totals_kernel,
        out_shape=(sums, sums, written, written),
        in_specs=[VMEM] * 4 + [ANY] * 2,
        out_specs=[ANY] * 4,
        scratch_shapes=[
            *[pltpu.VMEM((1, block_count), jnp.float32)] * 2,
            *[pltpu.SemaphoreType.DMA((2,))] * 2,
        ],
        input_output_aliases={4: 2, 5: 3},
        compiler_params=params(),
    )(parts, diagonal, less, great, *sigmas)
    sigma_l, sigma_g = [
        sigma.reshape(devices, block_count, row_count, orbitals) for sigma in sigmas
    ]
    return (sigma_l, sigma_g, current, ldos)


def solution(mesh):
    return jax.shard_map(
        local,
        mesh=mesh,
        in_specs=(
            P("energy", "space", None, None),
            P("energy", "space", None, None),
            P("energy", "space", None, None),
            P("space", None, None),
            P("energy", None),
            P(),
            P(),
        ),
        out_specs=(
            P(None, "space", "energy", None),
            P(None, "space", "energy", None),
            P("energy", "space"),
            P("energy", "space"),
        ),
        check_vma=False,
    )
```

```python
import functools

import jax
import jax.numpy as jnp
from jax import lax
from jax.experimental import pallas as pl
from jax.experimental.pallas import tpu as pltpu
from jax.sharding import PartitionSpec as P

phonon_occupation = 0.5

VMEM = pl.BlockSpec(memory_space=pltpu.VMEM)
SMEM = pl.BlockSpec(memory_space=pltpu.SMEM)
ANY = pl.BlockSpec(memory_space=pl.ANY)


def shifted(value, axis, steps):
    count = lax.axis_size(axis)
    initial, last = (max(0, -steps), min(count, count - steps))
    return lax.ppermute(value, axis, [(source, source + steps) for source in range(initial, last)])


def orders(count):
    def starting(root):
        return [root] + [index for index in range(count) if index != root]

    return starting(11 * count // 16), starting(count - 1)


def exchange(chunks, order):
    return lax.all_to_all(
        chunks, "energy", split_axis=0, concat_axis=0, tiled=True, axis_index_groups=[order]
    )


def params():
    return pltpu.CompilerParams(vmem_limit_bytes=24 * 1024 * 1024)


def product(left, right):
    return jnp.dot(left, right, preferred_element_type=jnp.float32)


def product_t(left, right):
    return lax.dot_general(
        left, right, (((1,), (1,)), ((), ())), preferred_element_type=jnp.float32
    )


def held(shape, dtype):
    return pltpu.VMEM(shape, dtype)


def in_hbm(*arrays):
    return [pltpu.with_memory_space_constraint(array, pltpu.HBM) for array in arrays]


def in_smem(array):
    return pltpu.with_memory_space_constraint(array, pltpu.SMEM)


def load_kernel(edges, *refs):
    inputs, active, shift = refs[:4], refs[4], refs[5]
    outputs, steps, open_mask, wide = refs[6:9], refs[9], refs[10], refs[11]
    packed, counts, sems = refs[12 : 12 + len(edges)], refs[-2], refs[-1]
    blocks = [ref if ref.ndim == 3 else ref.at[0] for ref in inputs]
    pairs = [(active, counts), (shift, steps)]
    for block_of, target in zip(edges, packed):
        block = block_of()
        pairs += [(ref.at[block], target.at[slot]) for slot, ref in enumerate(blocks)]
    pairs += list(zip((blocks[0], blocks[1], blocks[3]), outputs))
    copies = [
        pltpu.make_async_copy(origin, target, sems.at[index])
        for index, (origin, target) in enumerate(pairs)
    ]
    for copy in copies:
        copy.start()
    pad = wide.shape[0] // 4
    zeros = jnp.zeros((pad, *wide.shape[1:]), wide.dtype)
    wide[0:pad] = zeros
    wide[3 * pad :] = zeros
    for copy in copies:
        copy.wait()
    block_count = open_mask.shape[0]
    open_count = counts[lax.axis_index("energy")] - lax.axis_index("space") * block_count
    block_ids = lax.broadcasted_iota(jnp.int32, open_mask.shape, 0)
    open_mask[...] = (block_ids < open_count).astype(jnp.float32)


def load(edges, arrays, active, shift, devices):
    _, block_count, orbitals, _ = arrays[0].shape
    blocks = held((block_count, orbitals, orbitals), jnp.bfloat16)
    edge = held((len(arrays), orbitals, orbitals), jnp.bfloat16)
    copies = len(arrays) * (1 + len(edges)) + 2
    results = pl.pallas_call(
        functools.partial(load_kernel, edges),
        out_shape=(
            *[blocks] * 3,
            pltpu.SMEM(shift.shape, shift.dtype),
            held((block_count, orbitals), jnp.float32),
            held((2 * devices, 2, block_count * orbitals // devices, orbitals), jnp.float32),
            *[edge] * len(edges),
        ),
        in_specs=[ANY] * (len(arrays) + 2),
        out_specs=(*[VMEM] * 3, SMEM, VMEM, VMEM, *[VMEM] * len(edges)),
        scratch_shapes=[
            pltpu.SMEM(active.shape, active.dtype),
            pltpu.SemaphoreType.DMA((copies,)),
        ],
        compiler_params=params(),
    )(*in_hbm(*arrays, active, shift))
    kept = 3
    return results[:kept], results[kept : kept + 3], results[kept + 3 :]


def through(operator, less, great):
    rows = operator.shape[0]
    half = product(operator, jnp.concatenate([less, great], 1)).astype(jnp.bfloat16)
    stacked = jnp.concatenate([half[:, :rows], half[:, rows:]], 0)
    return product_t(stacked, operator)


def sandwiches(middles, green):
    orbitals = green.shape[1]
    halves, results = [], []
    for block, middle in enumerate(middles):
        middle = middle.astype(jnp.bfloat16)
        middle = jnp.concatenate([middle[:orbitals], middle[orbitals:]], 1)
        halves.append(product(green[block], middle).astype(jnp.bfloat16))
    for block, half in enumerate(halves):
        stacked = jnp.concatenate([half[:, :orbitals], half[:, orbitals:]], 0)
        results.append(product_t(stacked, green[block]))
    return results


def store(blocks, results, open_mask, outgoing, diagonal, order):
    orbitals = open_mask.shape[1]
    row_ids = lax.broadcasted_iota(jnp.int32, (orbitals, orbitals), 0)
    on_diagonal = row_ids == lax.broadcasted_iota(jnp.int32, (orbitals, orbitals), 1)
    kinds = {}
    for block in blocks:
        result = results[block] * open_mask[block : block + 1]
        kinds[block] = [result[:orbitals], result[orbitals:]]
        diagonal[block : block + 1] = jnp.sum(
            jnp.where(on_diagonal, kinds[block][0] + kinds[block][1], 0.0), axis=0, keepdims=True
        )
    for block in blocks:
        for kind in range(2):
            if order is None:
                outgoing[kind, block] = kinds[block][kind].astype(jnp.bfloat16)
            elif block % 2 == 0:
                rows = orbitals // len(order)
                for spot, device in enumerate(order):
                    piece = slice(device * rows, (device + 1) * rows)
                    pair = [kinds[block + step][kind][piece] for step in range(2)]
                    outgoing[spot, kind, block * rows : (block + 2) * rows] = jnp.concatenate(
                        pair, 0
                    ).astype(jnp.bfloat16)


def hop_kernel(outer, order, green, less, great, coupling, open_mask, partial, outgoing, diagonal):
    block_count, orbitals = green.shape[0], green.shape[1]
    blocks = range(block_count)
    hops, both, middles = [], [], []
    for block in blocks:
        factors = []
        if block + 1 < block_count:
            factors.append(coupling[block].T)
        if block > 0:
            factors.append(coupling[block - 1])
        hops.append(product(jnp.concatenate(factors, 0), green[block]).astype(jnp.bfloat16))
    for block in blocks:
        prior = jnp.concatenate([less[block], great[block]], 1)
        both.append(product(hops[block], prior).astype(jnp.bfloat16))
        middles.append(jnp.concatenate([less[block], great[block]], 0).astype(jnp.float32))
    for block in blocks:
        sent = []
        if block > 0:
            sent.append((block - 1, slice(0, orbitals)))
        if block + 1 < block_count:
            first = orbitals if block + 2 < block_count else 0
            sent.append((block + 1, slice(first, first + orbitals)))
        stacked = [
            jnp.concatenate([both[origin][piece, kind] for origin, piece in sent], 1)
            for kind in (slice(0, orbitals), slice(orbitals, 2 * orbitals))
        ]
        operators = jnp.concatenate([hops[origin][piece] for origin, piece in sent], 1)
        middles[block] = middles[block] + product_t(jnp.concatenate(stacked, 0), operators)
    results = sandwiches(middles, green)
    for slot, block in enumerate(outer):
        partial[slot] = results[block]
    inner = [block for block in blocks if block not in outer]
    store(inner, results, open_mask, outgoing, diagonal, order)


def edge_kernel(swap, outer, order, green, coupling, open_mask, partial, *rest):
    (_, inner_diagonal), halos, (outgoing, diagonal) = rest[:2], rest[2:-2], rest[-2:]
    last = green.shape[0] - 1
    place = lax.axis_index("space")
    results = {block: partial[slot] for slot, block in enumerate(outer)}

    def sent(retarded, hop, halo):
        operator = product(retarded, hop).astype(jnp.bfloat16)
        operator = product(operator, halo[0]).astype(jnp.bfloat16)
        return through(operator, halo[1], halo[2])

    if swap:
        (halo,) = halos
        retarded = jnp.where(place == 0, green[last], green[0])
        edge = sent(retarded, jnp.where(place == 0, coupling[last], halo[3].T), halo)
        results[0] = results[0] + jnp.where(place > 0, edge, 0.0)
        results[last] = results[last] + jnp.where(place == 0, edge, 0.0)
    elif halos:
        before, after = halos
        results[0] = results[0] + sent(green[0], before[3].T, before)
        results[last] = results[last] + sent(green[last], coupling[last], after)
    diagonal[...] = inner_diagonal[...]
    store(outer, results, open_mask, outgoing, diagonal, order)


def lane_sums(values):
    coarse = values.astype(jnp.bfloat16)
    fine = (values - coarse.astype(jnp.float32)).astype(jnp.bfloat16)
    ones = jnp.ones((8, 2 * values.shape[1]), jnp.bfloat16)
    return product_t(ones, jnp.concatenate([coarse, fine], 1))[0:1]


def copy_out(less, great, less_out, great_out, sems):
    copies = [
        pltpu.make_async_copy(less, less_out, sems.at[0]),
        pltpu.make_async_copy(great, great_out, sems.at[1]),
    ]
    for copy in copies:
        copy.start()
    for copy in copies:
        copy.wait()


def has_time():
    return lax.axis_index("energy") == 0


def totals_kernel(parts, diagonal, less, great, _, __, current, density, *outputs):
    total = parts[0]
    for spot in range(1, parts.shape[0]):
        total = total + parts[spot]
    current[...] = total
    density[...] = lane_sums(diagonal[...]) / diagonal.shape[1]
    pl.when(jnp.logical_not(has_time()))(functools.partial(copy_out, less, great, *outputs))


def spread(strength, rows):
    return jnp.concatenate([strength] * (rows // strength.shape[0]), 0)


def current_kernel(
    order, back_order, shift, rows, strength, _, parts, less, great, wide, *rest
):
    less_out, great_out, total, sems = rest
    energies, _, row_count, orbitals = rows.shape
    block_count = total.shape[1]
    pad = energies // 2
    for spot, energy in enumerate(order):
        wide[pad + energy] = rows[spot].astype(jnp.float32)
    factor = spread(strength[...], row_count)
    scale = spread(strength[...] * (1.0 / orbitals), row_count)
    first, second = shift[0], shift[1]

    def step(energy, carry):
        here = energy + pad
        above, below = (
            [wide[here + first, kind] + wide[here + second, kind] for kind in range(2)],
            [wide[here - first, kind] + wide[here - second, kind] for kind in range(2)],
        )
        gain = (1.0 + phonon_occupation) * above[0] + phonon_occupation * below[0]
        loss = (1.0 + phonon_occupation) * below[1] + phonon_occupation * above[1]
        less[energy] = (factor * gain).astype(less.dtype)
        great[energy] = (factor * loss).astype(great.dtype)
        flow = (gain * wide[here, 1] - loss * wide[here, 0]) * scale
        total[energy] = jnp.sum(flow.reshape(block_count, -1, orbitals), axis=1)
        return carry

    lax.fori_loop(0, energies, step, 0, unroll=4)
    flat = lane_sums(total[...].reshape(energies * block_count, orbitals))
    for spot, energy in enumerate(back_order):
        parts[spot] = flat[:, energy * block_count : (energy + 1) * block_count]
    pl.when(has_time())(functools.partial(copy_out, less, great, less_out, great_out, sems))


def local(
    green_ret, prior_less, prior_great, coupling, phonon_coupling, phonon_shift, active_blocks
):
    _, block_count, orbitals, _ = green_ret.shape
    devices, places = lax.axis_size("energy"), lax.axis_size("space")
    row_count = orbitals // devices
    last = block_count - 1
    order, back_order = orders(devices)
    swap = places == 2
    if swap:
        edges = [lambda: last * (1 - lax.axis_index("space"))]
    elif places > 1:
        edges = [lambda: last, lambda: 0]
    else:
        edges = []
    arrays, (shift, open_mask, wide), packed = load(
        edges,
        (green_ret, prior_less, prior_great, coupling),
        active_blocks,
        phonon_shift,
        devices,
    )
    green, less, coupling = arrays
    great = prior_great[0]
    if swap:
        halos = (lax.ppermute(packed[0], "space", [(0, 1), (1, 0)]),)
    else:
        halos = tuple(
            shifted(edge, "space", step) for edge, step in zip(packed, (1, -1), strict=False)
        )
    split = row_count % 8 == 0 and block_count % 2 == 0
    if split:
        out_shape = (devices, 2, block_count * row_count, orbitals)
    else:
        out_shape = (2, block_count, orbitals, orbitals)
    outer = sorted({0, 1, last - 1, last})
    store_order = order if split else None
    diagonals = held((block_count, orbitals), jnp.float32)
    partial, outgoing, diagonal = pl.pallas_call(
        functools.partial(hop_kernel, outer, store_order),
        out_shape=(
            held((len(outer), 2 * orbitals, orbitals), jnp.float32),
            held(out_shape, jnp.bfloat16),
            diagonals,
        ),
        in_specs=[VMEM] * 5,
        out_specs=(VMEM, VMEM, VMEM),
        compiler_params=params(),
        cost_estimate=pl.CostEstimate(
            flops=20 * block_count * orbitals**3,
            bytes_accessed=8 * block_count * orbitals**2,
            transcendentals=0,
        ),
    )(green, less, great, coupling, open_mask)
    outgoing, diagonal = pl.pallas_call(
        functools.partial(edge_kernel, swap, outer, store_order),
        out_shape=(held(out_shape, jnp.bfloat16), diagonals),
        in_specs=[VMEM] * (6 + len(halos)),
        out_specs=(VMEM, VMEM),
        input_output_aliases={4: 0},
        compiler_params=params(),
    )(green, coupling, open_mask, partial, outgoing, diagonal, *halos)
    if not split:
        outgoing = outgoing.reshape(2, block_count, devices, row_count, orbitals)
        outgoing = jnp.stack([outgoing[:, :, device] for device in order])
        outgoing = outgoing.reshape(devices, 2, block_count * row_count, orbitals)
    rows = exchange(outgoing, order)
    sigma_shape = (devices, block_count * row_count, orbitals)
    kept, written = held(sigma_shape, jnp.bfloat16), pltpu.HBM(sigma_shape, jnp.bfloat16)
    parts, less, great, _, *sigmas = pl.pallas_call(
        functools.partial(current_kernel, order, back_order),
        out_shape=(
            held((devices, 1, block_count), jnp.float32),
            kept,
            kept,
            held(wide.shape, wide.dtype),
            written,
            written,
        ),
        in_specs=[SMEM, VMEM, VMEM, VMEM],
        out_specs=(VMEM, VMEM, VMEM, VMEM, ANY, ANY),
        input_output_aliases={3: 3},
        scratch_shapes=[
            pltpu.VMEM((devices, block_count, orbitals), jnp.float32),
            pltpu.SemaphoreType.DMA((2,)),
        ],
        compiler_params=params(),
    )(in_smem(shift), rows, phonon_coupling, wide)
    parts = exchange(parts, back_order)
    sums = jax.ShapeDtypeStruct((1, block_count), jnp.float32)
    current, ldos, *sigmas = pl.pallas_call(
        totals_kernel,
        out_shape=(sums, sums, written, written),
        in_specs=[VMEM] * 4 + [ANY] * 2,
        out_specs=(VMEM, VMEM, ANY, ANY),
        scratch_shapes=[pltpu.SemaphoreType.DMA((2,))],
        input_output_aliases={4: 2, 5: 3},
        compiler_params=params(),
    )(parts, diagonal, less, great, *sigmas)
    sigma_l, sigma_g = [
        sigma.reshape(devices, block_count, row_count, orbitals) for sigma in sigmas
    ]
    return (sigma_l, sigma_g, current, ldos)


def solution(mesh):
    return jax.shard_map(
        local,
        mesh=mesh,
        in_specs=(
            P("energy", "space", None, None),
            P("energy", "space", None, None),
            P("energy", "space", None, None),
            P("space", None, None),
            P("energy", None),
            P(),
            P(),
        ),
        out_specs=(
            P(None, "space", "energy", None),
            P(None, "space", "energy", None),
            P("energy", "space"),
            P("energy", "space"),
        ),
        check_vma=False,
    )
```
